512 devices in a mesh: brick: 128 (over z, x, y_hi), rep: 4 (over y_lo, core).
Axes of the slice: x: 4, y: 4 (y_hi: 2, y_lo: 2; y = y_hi * 2 + y_lo), z: 16, core: 2. Of those that a mesh axis runs over, the one named last changes fastest.
Arguments:
- teacher_in: bfloat16 [4096, 6272], P('brick'), may hold values from -6 to 6
- student_in: bfloat16 [4096, 256], P('brick'), may hold values from -6 to 6
- wigner: bfloat16 [235, 65536], P(None, ('brick', 'rep')), may hold values from -2.390625 to 2.390625
- edge_basis: bfloat16 [65536, 128], P(('brick', 'rep')), may hold values from 0 to 1
- teacher_radial: bfloat16 [128, 128], replicated, may hold values from -0.5 to 0.5
- so2_m0: bfloat16 [896, 896], P('rep'), may hold values from -0.1875 to 0.1875
- so2_m1: bfloat16 [2, 768, 768], P(None, 'rep'), may hold values from -0.15625 to 0.15625
- so2_m2: bfloat16 [2, 640, 640], P(None, 'rep'), may hold values from -0.15625 to 0.15625
- w_src: bfloat16 [256, 256], replicated, may hold values from -0.375 to 0.375
- w_dst: bfloat16 [256, 256], replicated, may hold values from -0.375 to 0.375
- w_radial: bfloat16 [128, 256], replicated, may hold values from -0.5 to 0.5
- w_out: bfloat16 [256, 256], replicated, may hold values from -0.375 to 0.375
- w_head: bfloat16 [256, 128], replicated, may hold values from -0.375 to 0.375
- src: int32 [65536], P(('brick', 'rep')), may hold values from 0 to 63, as said below
- dst: int32 [65536], P(('brick', 'rep')), may hold values from 0 to 31, as said below
- edge_count: int32 [512], P(('brick', 'rep')), may hold values from 64 to 128, as said below
- atom_count: int32 [128], P('brick'), may hold values from 16 to 32, as said below
- send_idx: int32 [128, 2, 16], P('brick'), may hold values from 0 to 32, as said below
Outputs:
- teacher_out: bfloat16 [4096, 6272], P(('brick', 'rep'))
- grad_src: float32 [256, 256], replicated
- grad_dst: float32 [256, 256], replicated
- grad_radial: float32 [128, 256], replicated
- grad_out: float32 [256, 256], replicated
- grad_head: float32 [256, 128], replicated
The draws below stay inside these ranges and needn't reach their ends.
Inputs may be any that keep to these rules, and one draw needn't show every extreme that they name: `src`: for an edge of brick b: below atom_count[b] for an own atom, or 32 to 63 for a ghost slot. `dst`: below atom_count of the edge's brick. `edge_count`: some device's slots are all live. `atom_count`: some brick is full. `send_idx`: an own row below atom_count[b], or 32 for an empty slot; the last slot of every list is empty.
All inputs are finite; a program needn't handle non-finite values.
Results may differ from the reference program's by a relative error of at most 0.0039.
Values may be sent and summed in bfloat16 or wider, within the bound.
No kernel may reach another device: no remote copies, remote signals or barrier semaphores. Data moves between devices by JAX's collectives and lax.ppermute only.
A program may use at most 64 MiB of HBM per device.

```python
import math
import jax
import jax.numpy as jnp
from jax import lax

C = 128
LMAX = 6
MMAX = 2
SW = 256
RBF = 128
DEG = 16
OWN = 32
KC = 6272
NROT = 235
GHOST = 16
EDGE = 128
ATOMS = 4096
EDGES = 65536
N_BRICK = 128


def brick_counts(key):
    bricks = ATOMS // OWN
    first_key, second_key = jax.random.split(jax.random.fold_in(key, 7))
    counts = jax.random.randint(first_key, (bricks,), OWN // 2, OWN + 1, dtype=jnp.int32)
    fullest = jax.random.randint(second_key, (), 0, bricks, dtype=jnp.int32)
    return jnp.where(jnp.arange(bricks, dtype=jnp.int32) == fullest, OWN, counts).astype(jnp.int32)


def draw_atom_count(key, part):
    return brick_counts(key)


def draw_edge_count(key, part):
    devices_total = EDGES // EDGE
    first_key, second_key = jax.random.split(jax.random.fold_in(key, 19))
    counts = jax.random.randint(first_key, (devices_total,), EDGE // 2, EDGE + 1, dtype=jnp.int32)
    fullest = jax.random.randint(second_key, (), 0, devices_total, dtype=jnp.int32)
    return jnp.where(jnp.arange(devices_total, dtype=jnp.int32) == fullest, EDGE, counts).astype(jnp.int32)


def draw_send_idx(key, part):
    bricks = ATOMS // OWN
    counts = brick_counts(key)
    subkeys = jax.random.split(jax.random.fold_in(key, 23), 2)
    raw_rows = jax.random.randint(subkeys[0], (bricks, 2, GHOST), 0, 1 << 20, dtype=jnp.int32)
    rows_drawn = raw_rows % counts[:, None, None]
    empty_slot = jax.random.randint(subkeys[1], (bricks, 2, GHOST), 0, 4, dtype=jnp.int32) == 0
    chosen = jnp.where(empty_slot, OWN, rows_drawn)
    return chosen.at[:, :, GHOST - 1].set(OWN).astype(jnp.int32)


def edge_ends(key):
    bricks = ATOMS // OWN
    per_brick = EDGES // bricks
    counts = brick_counts(key)
    subkeys = jax.random.split(jax.random.fold_in(key, 31), 4)
    limits = counts[jnp.arange(EDGES, dtype=jnp.int32) // per_brick]
    own_side = jax.random.randint(subkeys[0], (EDGES,), 0, 1 << 20, dtype=jnp.int32) % limits
    ghost_side = OWN + jax.random.randint(subkeys[1], (EDGES,), 0, 2 * GHOST, dtype=jnp.int32)
    from_ghost = jax.random.randint(subkeys[2], (EDGES,), 0, 2, dtype=jnp.int32) == 0
    sources = jnp.where(from_ghost, ghost_side, own_side)
    targets = jax.random.randint(subkeys[3], (EDGES,), 0, 1 << 20, dtype=jnp.int32) % limits
    return (sources.astype(jnp.int32), targets.astype(jnp.int32))


def draw_src(key, part):
    return edge_ends(key)[0]


def draw_dst(key, part):
    return edge_ends(key)[1]


def steps_of(rng, dims, cuts, smallest, largest):
    gain = 1.0
    for position, blocks in cuts:
        heights = jax.random.uniform(jax.random.fold_in(jax.random.fold_in(rng, 6), position), (blocks,), jnp.float32, smallest / len(cuts), largest / len(cuts))
        gain = gain * jnp.repeat(jnp.exp(heights), dims[position] // blocks).reshape((-1,) + (1,) * (len(dims) - 1 - position))
    return gain


def normal_values(rng, shape, width, most, cuts=(), kind=jnp.bfloat16):
    drawn = jax.random.normal(rng, shape, jnp.float32) * width
    if len(cuts) > 0:
        drawn = steps_of(rng, shape, cuts, -0.22, 0.18) * drawn
    return jnp.clip(drawn, min=-most, max=most).astype(kind)


def setup_inputs(seed: int = 0) -> dict:
    key_list = jax.random.split(jax.random.key(seed), 19)
    teacher_in = normal_values(key_list[0], (ATOMS, KC), 1.0, 6.0, ((0, 128),))
    student_in = normal_values(key_list[1], (ATOMS, SW), 1.0, 6.0, ((0, 128),))
    wigner = normal_values(key_list[2], (NROT, EDGES), 0.4, 2.390625, ((1, 512),))
    edge_basis = jnp.clip(1.0 * jax.random.uniform(key_list[3], (EDGES, RBF), jnp.float32) ** steps_of(key_list[3], (EDGES, RBF), ((0, 512),), -0.2, 0.2), 0.0, 1.0).astype(jnp.bfloat16)
    teacher_radial = normal_values(key_list[4], (RBF, C), RBF ** -0.5, 0.5)
    so2_m0 = normal_values(key_list[5], (7 * C, 7 * C), (7 * C) ** -0.5, 0.1875, ((0, 4),))
    so2_m1 = normal_values(key_list[6], (2, 6 * C, 6 * C), (12 * C) ** -0.5, 0.15625, ((1, 4),))
    so2_m2 = normal_values(key_list[7], (2, 5 * C, 5 * C), (10 * C) ** -0.5, 0.15625, ((1, 4),))
    w_src = normal_values(key_list[8], (SW, SW), SW ** -0.5, 0.375)
    w_dst = normal_values(key_list[9], (SW, SW), SW ** -0.5, 0.375)
    w_radial = normal_values(key_list[10], (RBF, SW), RBF ** -0.5, 0.5)
    w_out = normal_values(key_list[11], (SW, SW), SW ** -0.5, 0.375)
    w_head = normal_values(key_list[12], (SW, C), SW ** -0.5, 0.375)
    src = draw_src(jax.random.fold_in(key_list[18], 71), 0)
    dst = draw_dst(jax.random.fold_in(key_list[18], 71), 0)
    edge_count = draw_edge_count(jax.random.fold_in(key_list[18], 71), 0)
    atom_count = draw_atom_count(jax.random.fold_in(key_list[18], 71), 0)
    send_idx = draw_send_idx(jax.random.fold_in(key_list[18], 71), 0)
    return {"teacher_in": teacher_in, "student_in": student_in, "wigner": wigner, "edge_basis": edge_basis, "teacher_radial": teacher_radial, "so2_m0": so2_m0, "so2_m1": so2_m1, "so2_m2": so2_m2, "w_src": w_src, "w_dst": w_dst, "w_radial": w_radial, "w_out": w_out, "w_head": w_head, "src": src, "dst": dst, "edge_count": edge_count, "atom_count": atom_count, "send_idx": send_idx}


def blocks_of(wig):
    blocks = []
    offset = 0
    for degree in range(LMAX + 1):
        order_cap = min(degree, MMAX)
        row_span = 2 * order_cap + 1
        col_span = 2 * degree + 1
        blocks.append(wig[offset:offset + row_span * col_span].reshape(row_span, col_span, wig.shape[1]))
        offset = offset + row_span * col_span
    return blocks

def rotate_into(sources, blocks, edge_gain):
    edge_total = sources.shape[0]
    coef_grid = sources.reshape(edge_total, (LMAX + 1) ** 2, -1).astype(jnp.float32)
    turned = []
    for degree in range(LMAX + 1):
        coeffs = coef_grid[:, degree * degree:(degree + 1) * (degree + 1), :]
        rotated = jnp.einsum('mje,ejc->emc', blocks[degree].astype(jnp.float32), coeffs)
        turned.append(rotated * edge_gain[:, None, :])
    centre = jnp.stack([turned[degree][:, min(degree, MMAX)] for degree in range(LMAX + 1)], axis=1)
    vectors = [centre.reshape(edge_total, -1).astype(jnp.bfloat16)]
    for morder in range(1, MMAX + 1):
        upper_part = jnp.stack([turned[degree][:, min(degree, MMAX) + morder] for degree in range(morder, LMAX + 1)], axis=1)
        lower_part = jnp.stack([turned[degree][:, min(degree, MMAX) - morder] for degree in range(morder, LMAX + 1)], axis=1)
        joined = jnp.concatenate([upper_part.reshape(edge_total, -1), lower_part.reshape(edge_total, -1)], axis=1)
        vectors.append(joined.astype(jnp.bfloat16))
    return vectors

def order_mixing(vectors, weights):
    results = [jnp.dot(vectors[0], weights[0], preferred_element_type=jnp.float32).astype(jnp.bfloat16)]
    for morder in range(1, MMAX + 1):
        half_cols = vectors[morder].shape[1] // 2
        plus_part = vectors[morder][:, :half_cols]
        minus_part = vectors[morder][:, half_cols:]
        real_part = weights[morder][0]
        imag_part = weights[morder][1]
        upper_out = jnp.dot(plus_part, real_part, preferred_element_type=jnp.float32) - jnp.dot(minus_part, imag_part, preferred_element_type=jnp.float32)
        lower_out = jnp.dot(plus_part, imag_part, preferred_element_type=jnp.float32) + jnp.dot(minus_part, real_part, preferred_element_type=jnp.float32)
        results.append(jnp.concatenate([upper_out, lower_out], axis=1).astype(jnp.bfloat16))
    return results

def rotate_back(outputs, blocks, edge_mask):
    edge_total = outputs[0].shape[0]
    centre = outputs[0].reshape(edge_total, LMAX + 1, -1)
    side_parts = [None]
    for morder in range(1, MMAX + 1):
        side_parts.append(outputs[morder].reshape(edge_total, 2, LMAX + 1 - morder, -1))
    pieces = []
    for degree in range(LMAX + 1):
        order_cap = min(degree, MMAX)
        entries = []
        for signed in range(-order_cap, order_cap + 1):
            if signed == 0:
                entries.append(centre[:, degree])
            elif signed > 0:
                entries.append(side_parts[signed][:, 0, degree - signed])
            else:
                entries.append(side_parts[-signed][:, 1, degree + signed])
        stacked = jnp.stack(entries, axis=1).astype(jnp.float32)
        pieces.append(jnp.einsum('mje,emc->ejc', blocks[degree].astype(jnp.float32), stacked))
    message = jnp.concatenate(pieces, axis=1) * edge_mask[:, None, None]
    return message.astype(jnp.bfloat16).reshape(edge_total, -1)

def reference(teacher_in, student_in, wigner, edge_basis, teacher_radial, so2_m0, so2_m1, so2_m2, w_src, w_dst, w_radial, w_out, w_head, src, dst, edge_count, atom_count, send_idx):
    brick_edges = EDGES // N_BRICK
    inv_degree = 1.0 / math.sqrt(DEG)
    inv_atoms = 1.0 / ATOMS
    weights = (so2_m0, so2_m1, so2_m2)
    teacher_pad = jnp.concatenate([teacher_in.reshape(N_BRICK, OWN, KC), jnp.zeros((N_BRICK, 1, KC), jnp.bfloat16)], axis=1)
    student_pad = jnp.concatenate([student_in.reshape(N_BRICK, OWN, SW), jnp.zeros((N_BRICK, 1, SW), jnp.bfloat16)], axis=1)
    slots = jnp.arange(EDGES, dtype=jnp.int32)
    live = (slots % EDGE < edge_count[slots // EDGE]).astype(jnp.float32).reshape(N_BRICK, brick_edges)
    src_all = src.reshape(N_BRICK, brick_edges)
    dst_all = dst.reshape(N_BRICK, brick_edges)
    wig_all = jnp.moveaxis(wigner.reshape(NROT, N_BRICK, brick_edges), 1, 0)
    basis_all = edge_basis.reshape(N_BRICK, brick_edges, RBF)

    def one_brick(totals, inputs):
        brick, src_e, dst_e, live_e, wig_e, basis_e = inputs
        left_brick = (brick + N_BRICK - 1) % N_BRICK
        right_brick = (brick + 1) % N_BRICK
        own_t = teacher_pad[brick][:OWN]
        own_s = student_pad[brick][:OWN]
        ext_t = jnp.concatenate([own_t, jnp.take(teacher_pad[left_brick], send_idx[left_brick, 0], axis=0), jnp.take(teacher_pad[right_brick], send_idx[right_brick, 1], axis=0)], axis=0)
        ext_s = jnp.concatenate([own_s, jnp.take(student_pad[left_brick], send_idx[left_brick, 0], axis=0), jnp.take(student_pad[right_brick], send_idx[right_brick, 1], axis=0)], axis=0)
        edge_gain = jnp.dot(basis_e, teacher_radial, preferred_element_type=jnp.float32)
        blocks = blocks_of(wig_e)
        vectors = rotate_into(jnp.take(ext_t, src_e, axis=0), blocks, edge_gain)
        outputs = order_mixing(vectors, weights)
        message = rotate_back(outputs, blocks, live_e)
        onehot = (dst_e[None, :] == jnp.arange(OWN, dtype=jnp.int32)[:, None]).astype(jnp.bfloat16)
        teacher_sum = jnp.dot(onehot, message, preferred_element_type=jnp.float32)
        teacher_rows = (own_t.astype(jnp.float32) + inv_degree * teacher_sum).astype(jnp.bfloat16)
        student_src = jnp.take(ext_s, src_e, axis=0)
        student_dst = jnp.take(own_s, dst_e, axis=0)
        hidden = jnp.dot(student_src, w_src, preferred_element_type=jnp.float32) + jnp.dot(student_dst, w_dst, preferred_element_type=jnp.float32) + jnp.dot(basis_e, w_radial, preferred_element_type=jnp.float32)
        gated_edges = (jax.nn.silu(hidden) * live_e[:, None]).astype(jnp.bfloat16)
        pooled = (jnp.dot(onehot, gated_edges, preferred_element_type=jnp.float32) * inv_degree).astype(jnp.bfloat16)
        updated = (own_s.astype(jnp.float32) + jnp.dot(pooled, w_out, preferred_element_type=jnp.float32)).astype(jnp.bfloat16)
        predicted = jnp.dot(updated, w_head, preferred_element_type=jnp.float32)
        atom_mask = (jnp.arange(OWN, dtype=jnp.int32) < atom_count[brick]).astype(jnp.float32)
        residual = (predicted - teacher_rows[:, :C].astype(jnp.float32)) * atom_mask[:, None]
        scaled = (residual * inv_atoms).astype(jnp.bfloat16)
        grad_head = jnp.dot(updated.T, scaled, preferred_element_type=jnp.float32)
        upstream = jnp.dot(scaled, w_head.T, preferred_element_type=jnp.float32).astype(jnp.bfloat16)
        grad_out = jnp.dot(pooled.T, upstream, preferred_element_type=jnp.float32)
        pooled_grad = jnp.dot(upstream, w_out.T, preferred_element_type=jnp.float32).astype(jnp.bfloat16)
        edge_grad = jnp.take(pooled_grad, dst_e, axis=0).astype(jnp.float32) * (inv_degree * live_e)[:, None]
        logistic = jax.nn.sigmoid(hidden)
        hidden_grad = (edge_grad * logistic * (1.0 + hidden * (1.0 - logistic))).astype(jnp.bfloat16)
        grad_src = jnp.dot(student_src.T, hidden_grad, preferred_element_type=jnp.float32)
        grad_dst = jnp.dot(student_dst.T, hidden_grad, preferred_element_type=jnp.float32)
        grad_radial = jnp.dot(basis_e.T, hidden_grad, preferred_element_type=jnp.float32)
        new_totals = (totals[0] + grad_src, totals[1] + grad_dst, totals[2] + grad_radial, totals[3] + grad_out, totals[4] + grad_head)
        return (new_totals, teacher_rows)
    start_totals = (jnp.zeros((SW, SW), jnp.float32), jnp.zeros((SW, SW), jnp.float32), jnp.zeros((RBF, SW), jnp.float32), jnp.zeros((SW, SW), jnp.float32), jnp.zeros((SW, C), jnp.float32))
    totals, teacher_blocks = lax.scan(one_brick, start_totals, (jnp.arange(N_BRICK, dtype=jnp.int32), src_all, dst_all, live, wig_all, basis_all))
    return (teacher_blocks.reshape(ATOMS, KC), totals[0], totals[1], totals[2], totals[3], totals[4])
```

```python
import functools
import math

import jax
import jax.numpy as jnp
from jax import lax
from jax.experimental import pallas as pl
from jax.experimental.pallas import tpu as pltpu
from jax.sharding import Mesh, PartitionSpec as P

LMAX = 6
MMAX = 2
DEG = 16
C = 128
OWN = 32
EXT = 64
EDGE = 128
SW = 256
KC = 6272
LOW = 7 * 224 + 6 * 192
HIGH = 6 * 192 + 10 * 160
SECTIONS = {0: (224, 0), 1: (192, 224), -1: (192, 416), 2: (160, 608), -2: (160, 768)}
BF = jnp.bfloat16
F32 = jnp.float32
BRICK = ("z", "x", "yh")
REP = ("yl", "core")
PLANE = ("x", "yh", "yl", "core")
VMEM = pl.BlockSpec(memory_space=pltpu.VMEM)
SMEM = pl.BlockSpec(memory_space=pltpu.SMEM)
PARAMS = pltpu.CompilerParams(vmem_limit_bytes=48 * 1024 * 1024)


def offsets():
    found = []
    row = 0
    for degree in range(LMAX + 1):
        found.append(row)
        row += (2 * min(degree, MMAX) + 1) * (2 * degree + 1)
    return found


OFFSET = offsets()


def dot(left, right, over=((1,), (0,))):
    return lax.dot_general(left, right, (over, ((), ())), preferred_element_type=F32)


def dst_onehot(dst_row):
    return dst_row == lax.broadcasted_iota(jnp.int32, (OWN, EDGE), 0)


def live_row(count):
    return lax.broadcasted_iota(jnp.int32, (1, EDGE), 1) < count


def live_col(count):
    return lax.broadcasted_iota(jnp.int32, (EDGE, 1), 0) < count


def send_body(lists_ref, teacher_ref, student_ref, next_ref, prev_ref):
    rows = lax.broadcasted_iota(jnp.int32, (32, OWN), 1)
    pick = (lists_ref[...] == rows).astype(BF)
    teacher = dot(pick, teacher_ref[...]).astype(BF)
    student = dot(pick, student_ref[...]).astype(BF)
    next_ref[:, :KC] = teacher[:16]
    prev_ref[:, :KC] = teacher[16:]
    next_ref[:, KC:] = student[:16]
    prev_ref[:, KC:] = student[16:]


def pack_body(m0_ref, m1_ref, m2_ref, all_ref, low_ref, high_ref):
    at = 0
    for part, wide, high in (
        (m0_ref, 7, 224), (m1_ref.at[0], 6, 192), (m1_ref.at[1], 6, 192),
        (m2_ref.at[0], 5, 160), (m2_ref.at[1], 5, 160),
    ):
        for n in range(wide):
            block = part[:, n * C : (n + 1) * C]
            all_ref[at : at + high] = block
            if at < LOW:
                low_ref[at : at + high] = block
            else:
                high_ref[at - LOW : at - LOW + high] = block
            at += high


def keep_turned(pack_ref, block, start, part, base):
    row = 0
    while row < C:
        which = (start + row) // part
        inside = (start + row) % part
        size = min(C - row, part - inside)
        pack_ref[which, base + inside : base + inside + size] = block[row : row + size]
        row += size


def front_body(
    count_ref, teacher_ref, left_ref, right_ref, student_ref, wig_ref, basis_ref, radial_ref,
    src_ref, dst_ref, m0_ref, wsrc_ref, wdst_ref, wrad_ref,
    pack_ref, small_ref, hidden_ref, ssrc_ref, sdst_ref,
    wigf_ref, turn_ref,
):
    count = count_ref[0]
    wigf_ref[...] = wig_ref[...].astype(F32)
    source = (src_ref[...] == lax.broadcasted_iota(jnp.int32, (EXT, EDGE), 0)).astype(F32)
    target = dst_onehot(dst_ref[...])
    basis = basis_ref[...]
    basis_t = basis.astype(F32).T.astype(BF)
    gain = dot(radial_ref[...], basis_t, ((0,), (0,)))
    for degree in range(LMAX + 1):
        cap = min(degree, MMAX)
        span = 2 * degree + 1
        orders = 2 * cap + 1
        for morder in range(orders):
            for j in range(span):
                row = OFFSET[degree] + morder * span + j
                turn_ref[j * EXT : (j + 1) * EXT, morder * EDGE : (morder + 1) * EDGE] = (
                    source * wigf_ref[row : row + 1, :]
                ).astype(BF)
        parts = []
        for j in range(span):
            lo = (degree * degree + j) * C
            parts += [
                teacher_ref[:, lo : lo + C],
                left_ref[:, lo : lo + C],
                right_ref[:, lo : lo + C],
            ]
        stacked = jnp.concatenate(parts, axis=0)
        turned = dot(stacked, turn_ref[: span * EXT, : orders * EDGE], ((0,), (0,)))
        for morder in range(orders):
            block = (turned[:, morder * EDGE : (morder + 1) * EDGE] * gain).astype(BF)
            signed = morder - cap
            part, base = SECTIONS[signed]
            keep_turned(pack_ref, block, (degree - abs(signed)) * C, part, base)
    invariant = dot(pack_ref[0, :224], m0_ref[0], ((0,), (0,)))
    for r in range(1, 4):
        invariant += dot(pack_ref[r, :224], m0_ref[r], ((0,), (0,)))
    live = live_row(count)
    scatter = jnp.where(target & live, wigf_ref[0:1, :], 0.0).astype(BF)
    student_ext = jnp.concatenate(
        [student_ref[...], left_ref[:, KC:], right_ref[:, KC:]], axis=0
    )
    ssrc = dot(source.astype(BF), student_ext, ((0,), (0,))).astype(BF)
    onehot = target.astype(F32).astype(BF)
    sdst = dot(onehot, student_ref[...], ((0,), (0,))).astype(BF)
    hidden = dot(ssrc, wsrc_ref[...]) + dot(sdst, wdst_ref[...]) + dot(basis, wrad_ref[...])
    gated = jnp.where(live_col(count), hidden * jax.nn.sigmoid(hidden), 0.0).astype(BF)
    small = jnp.concatenate(
        [dot(scatter, invariant.astype(BF)), dot(onehot, gated)], axis=1
    )
    for r in range(4):
        small_ref[r] = small
    hidden_ref[...] = hidden
    ssrc_ref[...] = ssrc
    sdst_ref[...] = sdst


def student_body(
    inv_atoms, count_ref, atoms_ref, rep_ref, smalls_ref, teacher_ref,
    student_ref, wout_ref, whead_ref, hidden_ref, ssrc_ref, sdst_ref, basis_ref, dst_ref,
    grad_ref,
):
    inv_degree = 1.0 / math.sqrt(DEG)
    sums = (smalls_ref[0] + smalls_ref[1]) + (smalls_ref[2] + smalls_ref[3])
    target = (teacher_ref[...].astype(F32) + inv_degree * sums[:, :C]).astype(BF)
    pooled = (sums[:, C:] * inv_degree).astype(BF)
    updated = (student_ref[...].astype(F32) + dot(pooled, wout_ref[...])).astype(BF)
    predicted = dot(updated, whead_ref[...])
    rows = lax.broadcasted_iota(jnp.int32, (OWN, 1), 0)
    residual = jnp.where(rows < atoms_ref[0], predicted - target.astype(F32), 0.0)
    scaled = (residual * inv_atoms).astype(BF)
    upstream = dot(scaled, whead_ref[...], ((1,), (1,))).astype(BF)
    lo = rep_ref[0] * 8
    mine = (rows >= lo) & (rows < lo + 8)
    scaled_part = jnp.where(mine, scaled.astype(F32), 0.0).astype(BF)
    upstream_part = jnp.where(mine, upstream.astype(F32), 0.0).astype(BF)
    grad_head = dot(updated, scaled_part, ((0,), (0,)))
    grad_out = dot(pooled, upstream_part, ((0,), (0,)))
    pooled_grad = dot(upstream, wout_ref[...], ((1,), (1,))).astype(BF)
    onehot = dst_onehot(dst_ref[...]).astype(F32).astype(BF)
    weight = jnp.where(live_col(count_ref[0]), inv_degree, 0.0)
    edge_grad = dot(onehot, pooled_grad, ((0,), (0,))) * weight
    hidden = hidden_ref[...]
    logistic = jax.nn.sigmoid(hidden)
    hidden_grad = (edge_grad * logistic * (1.0 + hidden * (1.0 - logistic))).astype(BF)
    for start, stop, value in (
        (0, 256, dot(ssrc_ref[...], hidden_grad, ((0,), (0,)))),
        (256, 512, dot(sdst_ref[...], hidden_grad, ((0,), (0,)))),
        (512, 768, grad_out),
        (768, 896, dot(basis_ref[...], hidden_grad, ((0,), (0,)))),
        (896, 1024, jnp.concatenate([grad_head[:C], grad_head[C:]], axis=1)),
    ):
        high = grad_ref.shape[1]
        grad_ref[start // high : stop // high] = value.astype(BF).reshape(-1, high, SW)


def spread_body(parts_ref, out_ref):
    total = parts_ref[0].astype(F32)
    for i in range(1, parts_ref.shape[0]):
        total += parts_ref[i].astype(F32)
    total = total.astype(out_ref.dtype)
    for i in range(out_ref.shape[0]):
        out_ref[i] = total


def unpack_body(all_ref, src_ref, dst_ref, radial_ref, out_ref, head_ref):
    values = all_ref[...].astype(F32).reshape(1024, SW)
    src_ref[...] = values[:256]
    dst_ref[...] = values[256:512]
    out_ref[...] = values[512:768]
    radial_ref[...] = values[768:896]
    head_ref[:C] = values[896:, :C]
    head_ref[C:] = values[896:, C:]


def blocks(ref, at, count, high):
    return jnp.concatenate(
        [ref[at + n * high : at + (n + 1) * high] for n in range(count)], axis=1
    )


def mix_body(
    count_ref, rep_ref, pack_ref, own_ref, near_ref, low_ref, high_ref, far_low_ref, far_high_ref,
    wig_ref, dst_ref,
    o0_ref, o1_ref, o2_ref, o3_ref,
    wigf_ref, back_ref, sums_ref,
):
    rep = rep_ref[0]
    live = live_row(count_ref[0])
    target = (dst_onehot(dst_ref[...]) & live).astype(F32)
    wigf_ref[...] = wig_ref[...].astype(F32)
    lows = (own_ref, near_ref, low_ref, far_low_ref)
    highs = (own_ref.at[LOW:], near_ref.at[LOW:], high_ref, far_high_ref)
    over = ((0,), (0,))
    y0 = 0.0
    for k in range(4):
        y0 += dot(pack_ref[rep ^ k, :224], blocks(lows[k], 0, 7, 224), over)
    y0 = y0.astype(BF)
    mixed = [None]
    for wide, base in ((6, 224), (5, 608)):
        size = wide * 32
        real = 0.0
        imag = 0.0
        for k in range(4):
            pair = jnp.concatenate(
                [
                    pack_ref[rep ^ k, base : base + size],
                    pack_ref[rep ^ k, base + size : base + 2 * size],
                ],
                axis=1,
            )
            if wide == 6:
                first = blocks(lows[k], 1568, 6, 192)
                second = blocks(highs[k], 0, 6, 192)
            else:
                first = blocks(highs[k], 1152, 5, 160)
                second = blocks(highs[k], 1952, 5, 160)
            real += dot(pair, first, over)
            imag += dot(pair, second, over)
        plus = (real[:EDGE] - imag[EDGE:]).astype(BF)
        minus = (imag[:EDGE] + real[EDGE:]).astype(BF)
        mixed.append((plus, minus))
    for degree in range(LMAX + 1):
        cap = min(degree, MMAX)
        span = 2 * degree + 1
        orders = 2 * cap + 1
        stacked = []
        for morder in range(orders):
            signed = morder - cap
            if signed == 0:
                stacked.append(y0[:, degree * C : (degree + 1) * C])
            else:
                slot = degree - abs(signed)
                part = mixed[abs(signed)][0 if signed > 0 else 1]
                stacked.append(part[:, slot * C : (slot + 1) * C])
            for j in range(span):
                row = OFFSET[degree] + morder * span + j
                back_ref[j * OWN : (j + 1) * OWN, morder * EDGE : (morder + 1) * EDGE] = (
                    target * wigf_ref[row : row + 1, :]
                ).astype(BF)
        summed = dot(
            back_ref[: span * OWN, : orders * EDGE], jnp.concatenate(stacked, axis=0)
        )
        for j in range(span):
            lo = (degree * degree + j) * C
            sums_ref[:, lo : lo + C] = summed[j * OWN : (j + 1) * OWN]
    for k, out_ref in enumerate((o0_ref, o1_ref, o2_ref, o3_ref)):
        start = pl.multiple_of((rep ^ k) * 8, 8)
        out_ref[...] = sums_ref[pl.ds(start, 8), :].astype(out_ref.dtype)


def finish_body(own_ref, s0_ref, s1_ref, s2_ref, s3_ref, out_ref):
    total = (s0_ref[...] + s1_ref[...].astype(F32)) + (
        s2_ref[...].astype(F32) + s3_ref[...].astype(F32)
    )
    out_ref[...] = (own_ref[...].astype(F32) + total * (1.0 / math.sqrt(DEG))).astype(BF)


def call(body, outs, ins, scratch=(), scalars=0):
    return pl.pallas_call(
        body,
        out_shape=tuple(jax.ShapeDtypeStruct(shape, dtype) for shape, dtype in outs),
        in_specs=[SMEM] * scalars + [VMEM] * (len(ins) - scalars),
        out_specs=tuple(VMEM for _ in outs),
        scratch_shapes=list(scratch),
        compiler_params=PARAMS,
    )(*ins)


def shifted(x, axes, by):
    length = lax.axis_size(axes)
    return lax.ppermute(x, axes, [(i, (i + by) % length) for i in range(length)])


def swapped(x, axes, mask):
    return lax.ppermute(x, axes, [(i, i ^ mask) for i in range(lax.axis_size(axes))])


def exchange(x, axes):
    return lax.all_to_all(x, axes, 0, 0, tiled=True)


def per_device(
    teacher_in, student_in, wigner, edge_basis, teacher_radial, so2_m0, so2_m1, so2_m2,
    w_src, w_dst, w_radial, w_out, w_head, src, dst, edge_count, atom_count, send_idx,
):
    bricks = lax.axis_size(BRICK)
    plane = lax.axis_size(PLANE)
    line = lax.axis_size("z")
    rep = lax.axis_index(REP).astype(jnp.int32)
    rep1 = rep.reshape(1)
    lists = send_idx.reshape(32, 1)
    to_next, to_prev = call(
        send_body, [((16, KC + SW), BF)] * 2, (lists, teacher_in, student_in)
    )
    from_left = shifted(to_next, BRICK, 1)
    from_right = shifted(to_prev, BRICK, -1)
    own, low, high = call(
        pack_body,
        [((LOW + HIGH, C), BF), ((LOW, C), BF), ((HIGH, C), BF)],
        (so2_m0, so2_m1, so2_m2),
    )
    column = exchange(jnp.broadcast_to(so2_m0[None, :, :C], (4, 224, C)), REP)
    near = swapped(own, "core", 1)
    across_low = shifted(low, ("yh", "yl"), 1)
    across_high = shifted(high, ("yh", "yl"), -1)
    far_low = swapped(across_low, "core", 1)
    far_high = swapped(across_high, "core", 1)
    src_row = src.reshape(1, EDGE)
    dst_row = dst.reshape(1, EDGE)
    pack, small, hidden, ssrc, sdst = call(
        front_body,
        [
            ((4, 928, EDGE), BF), ((4, OWN, C + SW), F32), ((EDGE, SW), F32),
            ((EDGE, SW), BF), ((EDGE, SW), BF),
        ],
        (
            edge_count, teacher_in, from_left, from_right, student_in, wigner, edge_basis,
            teacher_radial, src_row, dst_row, column, w_src, w_dst, w_radial,
        ),
        [pltpu.VMEM((235, EDGE), F32), pltpu.VMEM((13 * EXT, 5 * EDGE), BF)],
        1,
    )
    smalls = exchange(small, REP)
    (grads,) = call(
        functools.partial(student_body, 1.0 / (OWN * bricks)),
        [((plane, 1024 // plane, SW), BF)],
        (
            edge_count, atom_count, rep1, smalls, teacher_in[:, :C], student_in, w_out, w_head,
            hidden, ssrc, sdst, edge_basis, dst_row,
        ),
        (),
        3,
    )
    plane_parts = exchange(grads, PLANE)
    (plane_sum,) = call(spread_body, [((line, 1024 // plane, SW), BF)], (plane_parts,))
    shares = call(
        mix_body,
        [((8, KC), F32)] + [((8, KC), BF)] * 3,
        (
            edge_count, rep1, pack, own, near, across_low, across_high, far_low, far_high,
            wigner, dst_row,
        ),
        [
            pltpu.VMEM((235, EDGE), F32),
            pltpu.VMEM((13 * OWN, 5 * EDGE), BF),
            pltpu.VMEM((OWN, KC), F32),
        ],
        2,
    )
    arrived = [shares[0]] + [swapped(shares[k], REP, k) for k in (1, 2, 3)]
    line_parts = exchange(plane_sum, "z")
    (total,) = call(spread_body, [((plane, 1024 // plane, SW), BF)], (line_parts,))
    totals = exchange(total, PLANE)
    grads_out = call(
        unpack_body,
        [((256, SW), F32), ((256, SW), F32), ((128, SW), F32), ((256, SW), F32), ((256, C), F32)],
        (totals,),
    )
    mine = lax.dynamic_slice_in_dim(teacher_in, rep * 8, 8, 0)
    (teacher_out,) = call(finish_body, [((8, KC), BF)], (mine, *arrived))
    return (teacher_out, *grads_out)


def solution(mesh):
    fine = Mesh(mesh.devices.reshape(16, 4, 2, 2, 2), BRICK + REP)
    every = BRICK + REP
    placed = (
        P(BRICK, None),
        P(BRICK, None),
        P(None, every),
        P(every, None),
        P(),
        P(REP, None),
        P(None, REP, None),
        P(None, REP, None),
        P(),
        P(),
        P(),
        P(),
        P(),
        P(every),
        P(every),
        P(every),
        P(BRICK),
        P(BRICK, None, None),
    )
    return jax.shard_map(
        per_device,
        mesh=fine,
        in_specs=placed,
        out_specs=(P(every, None), P(), P(), P(), P(), P()),
        check_vma=False,
    )
```

```python
import functools
import math

import jax
import jax.numpy as jnp
from jax import lax
from jax.experimental import pallas as pl
from jax.experimental.pallas import tpu as pltpu
from jax.sharding import Mesh, PartitionSpec as P

LMAX = 6
MMAX = 2
DEG = 16
C = 128
OWN = 32
EXT = 64
EDGE = 128
SW = 256
KC = 6272
FULL = 64 << 10
FRONT = 1024
LOW = 7 * 224 + 6 * 192
HIGH = 6 * 192 + 10 * 160
SECTIONS = {0: (224, 0), 1: (192, 224), -1: (192, 416), 2: (160, 608), -2: (160, 768)}
BF = jnp.bfloat16
F32 = jnp.float32
BRICK = ("z", "x", "yh")
REP = ("yl", "core")
PLANE = ("x", "yh", "yl", "core")
VMEM = pl.BlockSpec(memory_space=pltpu.VMEM)
HBM = pl.BlockSpec(memory_space=pltpu.HBM)
ANY = pl.BlockSpec(memory_space=pl.ANY)
SMEM = pl.BlockSpec(memory_space=pltpu.SMEM)


def offsets():
    found = []
    row = 0
    for degree in range(LMAX + 1):
        found.append(row)
        row += (2 * min(degree, MMAX) + 1) * (2 * degree + 1)
    return found


OFFSET = offsets()


def dot(left, right, over=((1,), (0,))):
    return lax.dot_general(left, right, (over, ((), ())), preferred_element_type=F32)


def dst_onehot(dst_row):
    return dst_row == lax.broadcasted_iota(jnp.int32, (OWN, EDGE), 0)


def live_row(count):
    return lax.broadcasted_iota(jnp.int32, (1, EDGE), 1) < count


def live_col(count):
    return lax.broadcasted_iota(jnp.int32, (EDGE, 1), 0) < count


def fetch(pairs, sems):
    copies = [
        pltpu.make_async_copy(source, target, sems.at[i])
        for i, (source, target) in enumerate(pairs)
    ]
    for copy in copies:
        copy.start()
    return copies


def start_body(
    lists_hbm, teacher_hbm, student_hbm, m0_hbm,
    next_ref, prev_ref, column_ref,
    lists_ref, teacher_ref, student_ref, m0_ref, sems,
):
    copies = fetch(
        (
            (lists_hbm, lists_ref), (teacher_hbm, teacher_ref), (student_hbm, student_ref),
            (m0_hbm.at[:, :C], m0_ref),
        ),
        sems,
    )
    for copy in copies:
        copy.wait()
    rows = lax.broadcasted_iota(jnp.int32, (OWN, 16), 0)
    for k, out_ref in enumerate((next_ref, prev_ref)):
        pick = (rows == lists_ref[0, k : k + 1, :]).astype(F32).astype(BF)
        out_ref[:, :KC] = dot(pick, teacher_ref[...], ((0,), (0,))).astype(BF)
        out_ref[:, KC:] = dot(pick, student_ref[...], ((0,), (0,))).astype(BF)
    for r in range(4):
        column_ref[r] = m0_ref[...]


def pack_body(
    m0_hbm, m1_hbm, m2_hbm, all_ref, low_ref, high_ref, m0_ref, m1_ref, m2_ref, sems
):
    copies = fetch(((m0_hbm, m0_ref), (m1_hbm, m1_ref), (m2_hbm, m2_ref)), sems)
    at = 0
    for part, wide, high, ready in (
        (m0_ref, 7, 224, 0), (m1_ref.at[0], 6, 192, 1), (m1_ref.at[1], 6, 192, None),
        (m2_ref.at[0], 5, 160, 2), (m2_ref.at[1], 5, 160, None),
    ):
        if ready is not None:
            copies[ready].wait()
        for n in range(wide):
            block = part[:, n * C : (n + 1) * C]
            all_ref[at : at + high] = block
            if at < LOW:
                low_ref[at : at + high] = block
            else:
                high_ref[at - LOW : at - LOW + high] = block
            at += high


def keep_turned(pack_ref, block, start, part, base):
    row = 0
    while row < C:
        which = (start + row) // part
        inside = (start + row) % part
        size = min(C - row, part - inside)
        pack_ref[which, base + inside : base + inside + size] = block[row : row + size]
        row += size


def front_body(
    count_ref, left_ref, right_ref, m0_ref, *refs
):
    raw = refs[:10]
    pack_ref, small_ref, hidden_ref, ssrc_ref, sdst_ref = refs[10:15]
    held = refs[15:25]
    wigf_ref, turn_ref, sems = refs[25:]
    (
        teacher_ref, student_ref, wig_ref, basis_ref, radial_ref, src_ref, dst_ref, wsrc_ref,
        wdst_ref, wrad_ref,
    ) = held
    for copy in fetch(tuple(zip(raw, held)), sems):
        copy.wait()
    count = count_ref[0]
    wigf_ref[...] = wig_ref[...].astype(F32)
    source = (src_ref[...] == lax.broadcasted_iota(jnp.int32, (EXT, EDGE), 0)).astype(F32)
    target = dst_onehot(dst_ref[...])
    basis = basis_ref[...]
    basis_t = basis.astype(F32).T.astype(BF)
    gain = dot(radial_ref[...], basis_t, ((0,), (0,)))
    for degree in range(LMAX + 1):
        cap = min(degree, MMAX)
        span = 2 * degree + 1
        orders = 2 * cap + 1
        for morder in range(orders):
            for j in range(span):
                row = OFFSET[degree] + morder * span + j
                turn_ref[j * EXT : (j + 1) * EXT, morder * EDGE : (morder + 1) * EDGE] = (
                    source * wigf_ref[row : row + 1, :]
                ).astype(BF)
        parts = []
        for j in range(span):
            lo = (degree * degree + j) * C
            parts += [
                teacher_ref[:, lo : lo + C],
                left_ref[:, lo : lo + C],
                right_ref[:, lo : lo + C],
            ]
        stacked = jnp.concatenate(parts, axis=0)
        turned = dot(stacked, turn_ref[: span * EXT, : orders * EDGE], ((0,), (0,)))
        for morder in range(orders):
            block = (turned[:, morder * EDGE : (morder + 1) * EDGE] * gain).astype(BF)
            signed = morder - cap
            part, base = SECTIONS[signed]
            keep_turned(pack_ref, block, (degree - abs(signed)) * C, part, base)
    student_ext = jnp.concatenate(
        [student_ref[...], left_ref[:, KC:], right_ref[:, KC:]], axis=0
    )
    ssrc = dot(source.astype(BF), student_ext, ((0,), (0,))).astype(BF)
    onehot = target.astype(F32).astype(BF)
    sdst = dot(onehot, student_ref[...], ((0,), (0,))).astype(BF)
    hidden = dot(ssrc, wsrc_ref[...]) + dot(sdst, wdst_ref[...]) + dot(basis, wrad_ref[...])
    gated = jnp.where(live_col(count), hidden * jax.nn.sigmoid(hidden), 0.0).astype(BF)
    invariant = dot(pack_ref[0, :224], m0_ref[0], ((0,), (0,)))
    for r in range(1, 4):
        invariant += dot(pack_ref[r, :224], m0_ref[r], ((0,), (0,)))
    keep = target & live_row(count)
    scatter = jnp.where(keep, wigf_ref[0:1, :], 0.0).astype(BF)
    sums = dot(scatter, invariant.astype(BF))
    pooled = dot(onehot, gated)
    for r in range(4):
        small_ref[r, :, :C] = sums
        small_ref[r, :, C:] = pooled
    hidden_ref[...] = hidden
    ssrc_ref[...] = ssrc
    sdst_ref[...] = sdst


def student_body(inv_atoms, count_ref, atoms_ref, rep_ref, *refs):
    raw = list(refs[:10])
    raw[1] = raw[1].at[:, :C]
    grad_ref = refs[10]
    held = refs[11:21]
    (
        smalls_ref, teacher_ref, student_ref, wout_ref, whead_ref, hidden_ref, ssrc_ref,
        sdst_ref, basis_ref, dst_ref,
    ) = held
    for copy in fetch(tuple(zip(raw, held)), refs[21]):
        copy.wait()
    inv_degree = 1.0 / math.sqrt(DEG)
    sums = (smalls_ref[0] + smalls_ref[1]) + (smalls_ref[2] + smalls_ref[3])
    target = (teacher_ref[...].astype(F32) + inv_degree * sums[:, :C]).astype(BF)
    pooled = (sums[:, C:] * inv_degree).astype(BF)
    updated = (student_ref[...].astype(F32) + dot(pooled, wout_ref[...])).astype(BF)
    predicted = dot(updated, whead_ref[...])
    rows = lax.broadcasted_iota(jnp.int32, (OWN, 1), 0)
    residual = jnp.where(rows < atoms_ref[0], predicted - target.astype(F32), 0.0)
    scaled = (residual * inv_atoms).astype(BF)
    upstream = dot(scaled, whead_ref[...], ((1,), (1,))).astype(BF)
    lo = rep_ref[0] * 8
    mine = (rows >= lo) & (rows < lo + 8)
    scaled_part = jnp.where(mine, scaled.astype(F32), 0.0).astype(BF)
    upstream_part = jnp.where(mine, upstream.astype(F32), 0.0).astype(BF)
    grad_head = dot(updated, scaled_part, ((0,), (0,)))
    grad_out = dot(pooled, upstream_part, ((0,), (0,)))
    pooled_grad = dot(upstream, wout_ref[...], ((1,), (1,))).astype(BF)
    onehot = dst_onehot(dst_ref[...]).astype(F32).astype(BF)
    weight = jnp.where(live_col(count_ref[0]), inv_degree, 0.0)
    edge_grad = dot(onehot, pooled_grad, ((0,), (0,))) * weight
    hidden = hidden_ref[...]
    logistic = jax.nn.sigmoid(hidden)
    hidden_grad = (edge_grad * logistic * (1.0 + hidden * (1.0 - logistic))).astype(BF)
    for start, stop, value in (
        (0, 256, dot(ssrc_ref[...], hidden_grad, ((0,), (0,)))),
        (256, 512, dot(sdst_ref[...], hidden_grad, ((0,), (0,)))),
        (512, 768, grad_out),
        (768, 896, dot(basis_ref[...], hidden_grad, ((0,), (0,)))),
        (896, 1024, jnp.concatenate([grad_head[:C], grad_head[C:]], axis=1)),
    ):
        high = grad_ref.shape[1]
        grad_ref[start // high : stop // high] = value.astype(BF).reshape(-1, high, SW)


def spread_body(parts_ref, *refs):
    out_ref = refs[-1]
    total = parts_ref[0].astype(F32)
    for i in range(1, parts_ref.shape[0]):
        total += parts_ref[i].astype(F32)
    total = total.astype(out_ref.dtype)
    for i in range(out_ref.shape[0]):
        out_ref[i] = total


def unpack_body(all_ref, src_ref, dst_ref, radial_ref, out_ref, head_ref):
    values = all_ref[...].astype(F32).reshape(1024, SW)
    src_ref[...] = values[:256]
    dst_ref[...] = values[256:512]
    out_ref[...] = values[512:768]
    radial_ref[...] = values[768:896]
    head_ref[:C] = values[896:, :C]
    head_ref[C:] = values[896:, C:]


def blocks(ref, at, count, high):
    return jnp.concatenate(
        [ref[at + n * high : at + (n + 1) * high] for n in range(count)], axis=1
    )


def mix_body(
    count_ref, rep_ref, pack_ref, own_ref, near_ref, low_ref, high_ref, far_low_ref, far_high_ref,
    wig_ref, dst_ref, after_ref,
    o0_ref, o1_ref, o2_ref, o3_ref,
    wigf_ref, back_ref, sums_ref,
):
    rep = rep_ref[0]
    live = live_row(count_ref[0])
    target = (dst_onehot(dst_ref[...]) & live).astype(F32)
    wigf_ref[...] = wig_ref[...].astype(F32)
    lows = (own_ref, near_ref, low_ref, far_low_ref)
    highs = (own_ref.at[LOW:], near_ref.at[LOW:], high_ref, far_high_ref)
    over = ((0,), (0,))
    y0 = 0.0
    for k in range(4):
        y0 += dot(pack_ref[rep ^ k, :224], blocks(lows[k], 0, 7, 224), over)
    y0 = y0.astype(BF)
    mixed = [None]
    for wide, base in ((6, 224), (5, 608)):
        size = wide * 32
        real = 0.0
        imag = 0.0
        for k in range(4):
            pair = jnp.concatenate(
                [
                    pack_ref[rep ^ k, base : base + size],
                    pack_ref[rep ^ k, base + size : base + 2 * size],
                ],
                axis=1,
            )
            if wide == 6:
                first = blocks(lows[k], 1568, 6, 192)
                second = blocks(highs[k], 0, 6, 192)
            else:
                first = blocks(highs[k], 1152, 5, 160)
                second = blocks(highs[k], 1952, 5, 160)
            real += dot(pair, first, over)
            imag += dot(pair, second, over)
        plus = (real[:EDGE] - imag[EDGE:]).astype(BF)
        minus = (imag[:EDGE] + real[EDGE:]).astype(BF)
        mixed.append((plus, minus))
    for degree in range(LMAX + 1):
        cap = min(degree, MMAX)
        span = 2 * degree + 1
        orders = 2 * cap + 1
        stacked = []
        for morder in range(orders):
            signed = morder - cap
            if signed == 0:
                stacked.append(y0[:, degree * C : (degree + 1) * C])
            else:
                slot = degree - abs(signed)
                part = mixed[abs(signed)][0 if signed > 0 else 1]
                stacked.append(part[:, slot * C : (slot + 1) * C])
            for j in range(span):
                row = OFFSET[degree] + morder * span + j
                back_ref[j * OWN : (j + 1) * OWN, morder * EDGE : (morder + 1) * EDGE] = (
                    target * wigf_ref[row : row + 1, :]
                ).astype(BF)
        summed = dot(
            back_ref[: span * OWN, : orders * EDGE], jnp.concatenate(stacked, axis=0)
        )
        for j in range(span):
            lo = (degree * degree + j) * C
            sums_ref[:, lo : lo + C] = summed[j * OWN : (j + 1) * OWN]
    for k, out_ref in enumerate((o0_ref, o1_ref, o2_ref, o3_ref)):
        start = pl.multiple_of((rep ^ k) * 8, 8)
        out_ref[...] = sums_ref[pl.ds(start, 8), :].astype(out_ref.dtype)


def finish_body(own_ref, s0_ref, s1_ref, s2_ref, s3_ref, out_ref):
    total = (s0_ref[...] + s1_ref[...].astype(F32)) + (
        s2_ref[...].astype(F32) + s3_ref[...].astype(F32)
    )
    out_ref[...] = (own_ref[...].astype(F32) + total * (1.0 / math.sqrt(DEG))).astype(BF)


def call(body, outs, ins, scratch=(), scalars=0, raws=0, after=0, flops=0, room=24 << 10):
    specs = [SMEM] * scalars + [VMEM] * (len(ins) - scalars - raws - after)
    return pl.pallas_call(
        body,
        out_shape=tuple(jax.ShapeDtypeStruct(shape, dtype) for shape, dtype in outs),
        in_specs=specs + [HBM] * raws + [ANY] * after,
        out_specs=tuple(VMEM for _ in outs),
        scratch_shapes=list(scratch),
        compiler_params=pltpu.CompilerParams(vmem_limit_bytes=(FULL - room) << 10),
        cost_estimate=pl.CostEstimate(flops=flops, bytes_accessed=4096, transcendentals=0),
    )(*ins)


def held(arrays):
    return [pltpu.VMEM(array.shape, array.dtype) for array in arrays]


def shifted(x, axes, by):
    length = lax.axis_size(axes)
    return lax.ppermute(x, axes, [(i, (i + by) % length) for i in range(length)])


def swapped(x, axes, mask):
    return lax.ppermute(x, axes, [(i, i ^ mask) for i in range(lax.axis_size(axes))])


def exchange(x, axes):
    return lax.all_to_all(x, axes, 0, 0, tiled=True)


def per_device(
    teacher_in, student_in, wigner, edge_basis, teacher_radial, so2_m0, so2_m1, so2_m2,
    w_src, w_dst, w_radial, w_out, w_head, src, dst, edge_count, atom_count, send_idx,
):
    bricks = lax.axis_size(BRICK)
    plane = lax.axis_size(PLANE)
    line = lax.axis_size("z")
    rep = lax.axis_index(REP).astype(jnp.int32)
    rep1 = rep.reshape(1)
    src_row = src.reshape(1, EDGE)
    dst_row = dst.reshape(1, EDGE)
    to_next, to_prev, own_column = call(
        start_body,
        [((16, KC + SW), BF), ((16, KC + SW), BF), ((4, 224, C), BF)],
        (send_idx, teacher_in, student_in, so2_m0),
        held((send_idx, teacher_in, student_in))
        + [pltpu.VMEM((224, C), BF), pltpu.SemaphoreType.DMA((4,))],
        raws=4,
        room=1024,
    )
    from_left = shifted(to_next, BRICK, 1)
    from_right = shifted(to_prev, BRICK, -1)
    column = exchange(own_column, REP)
    raw = (
        teacher_in, student_in, wigner, edge_basis, teacher_radial, src_row, dst_row, w_src,
        w_dst, w_radial,
    )
    pack, small, hidden, ssrc, sdst = call(
        front_body,
        [
            ((4, 928, EDGE), BF), ((4, OWN, C + SW), F32), ((EDGE, SW), F32),
            ((EDGE, SW), BF), ((EDGE, SW), BF),
        ],
        (edge_count, from_left, from_right, column, *raw),
        held(raw)
        + [
            pltpu.VMEM((235, EDGE), F32), pltpu.VMEM((13 * EXT, 5 * EDGE), BF),
            pltpu.SemaphoreType.DMA((10,)),
        ],
        scalars=1,
        raws=10,
        flops=1 << 31,
        room=FRONT,
    )
    smalls = exchange(small, REP)
    mixings = (so2_m0, so2_m1, so2_m2)
    own, low, high = call(
        pack_body,
        [((LOW + HIGH, C), BF), ((LOW, C), BF), ((HIGH, C), BF)],
        mixings,
        held(mixings) + [pltpu.SemaphoreType.DMA((3,))],
        raws=3,
        room=1024,
        flops=1 << 30,
    )
    near = swapped(own, "core", 1)
    across_low = shifted(low, ("yh", "yl"), 1)
    across_high = shifted(high, ("yh", "yl"), -1)
    far_low = swapped(across_low, "core", 1)
    far_high = swapped(across_high, "core", 1)
    raw = (
        smalls, teacher_in, student_in, w_out, w_head, hidden, ssrc, sdst, edge_basis, dst_row,
    )
    (grads,) = call(
        functools.partial(student_body, 1.0 / (OWN * bricks)),
        [((plane, 1024 // plane, SW), BF)],
        (edge_count, atom_count, rep1, *raw),
        held((smalls,))
        + [pltpu.VMEM((OWN, C), BF)]
        + held(raw[2:])
        + [pltpu.SemaphoreType.DMA((10,))],
        scalars=3,
        raws=10,
        flops=1 << 30,
        room=1024,
    )
    plane_parts = exchange(grads, PLANE)
    (plane_sum,) = call(spread_body, [((line, 1024 // plane, SW), BF)], (plane_parts,))
    shares = call(
        mix_body,
        [((8, KC), F32)] + [((8, KC), BF)] * 3,
        (
            edge_count, rep1, pack, own, near, across_low, across_high, far_low, far_high,
            wigner, dst_row, plane_sum,
        ),
        [
            pltpu.VMEM((235, EDGE), F32),
            pltpu.VMEM((13 * OWN, 5 * EDGE), BF),
            pltpu.VMEM((OWN, KC), F32),
        ],
        scalars=2,
        after=1,
        flops=1 << 32,
    )
    line_parts = exchange(plane_sum, "z")
    (total,) = call(
        spread_body, [((plane, 1024 // plane, SW), BF)], (line_parts, shares[0]), after=1
    )
    totals = exchange(total, PLANE)
    arrived = [shares[0]] + [swapped(shares[k], REP, k) for k in (1, 2, 3)]
    mine = lax.dynamic_slice_in_dim(teacher_in, rep * 8, 8, 0)
    (teacher_out,) = call(finish_body, [((8, KC), BF)], (mine, *arrived))
    grads_out = call(
        unpack_body,
        [((256, SW), F32), ((256, SW), F32), ((128, SW), F32), ((256, SW), F32), ((256, C), F32)],
        (totals,),
    )
    return (teacher_out, *grads_out)


def solution(mesh):
    fine = Mesh(mesh.devices.reshape(16, 4, 2, 2, 2), BRICK + REP)
    every = BRICK + REP
    placed = (
        P(BRICK, None),
        P(BRICK, None),
        P(None, every),
        P(every, None),
        P(),
        P(REP, None),
        P(None, REP, None),
        P(None, REP, None),
        P(),
        P(),
        P(),
        P(),
        P(),
        P(every),
        P(every),
        P(every),
        P(BRICK),
        P(BRICK, None, None),
    )
    return jax.shard_map(
        per_device,
        mesh=fine,
        in_specs=placed,
        out_specs=(P(every, None), P(), P(), P(), P(), P()),
        check_vma=False,
    )
```

```python
import functools
import math

import jax
import jax.numpy as jnp
from jax import lax
from jax.experimental import pallas as pl
from jax.experimental.pallas import tpu as pltpu
from jax.sharding import Mesh, PartitionSpec as P

LMAX = 6
MMAX = 2
DEG = 16
C = 128
OWN = 32
EXT = 64
EDGE = 128
SW = 256
KC = 6272
FULL = 64 << 10
LOW = 7 * 224 + 6 * 192
HIGH = 6 * 192 + 10 * 160
SECTIONS = {0: (224, 0), 1: (192, 224), -1: (192, 416), 2: (160, 608), -2: (160, 768)}
BF = jnp.bfloat16
F32 = jnp.float32
BRICK = ("z", "x", "yh")
REP = ("yl", "core")
PLANE = ("x", "yh", "yl", "core")
VMEM = pl.BlockSpec(memory_space=pltpu.VMEM)
HBM = pl.BlockSpec(memory_space=pltpu.HBM)
ANY = pl.BlockSpec(memory_space=pl.ANY)
SMEM = pl.BlockSpec(memory_space=pltpu.SMEM)


def offsets():
    found = []
    row = 0
    for degree in range(LMAX + 1):
        found.append(row)
        row += (2 * min(degree, MMAX) + 1) * (2 * degree + 1)
    return found


OFFSET = offsets()


def dot(left, right, over=((1,), (0,))):
    return lax.dot_general(left, right, (over, ((), ())), preferred_element_type=F32)


def live_row(count):
    return lax.broadcasted_iota(jnp.int32, (1, EDGE), 1) < count


def fetch(pairs, sems):
    copies = [
        pltpu.make_async_copy(source, target, sems.at[i])
        for i, (source, target) in enumerate(pairs)
    ]
    for copy in copies:
        copy.start()
    return copies


def start_body(
    count_ref, lists_hbm, teacher_hbm, student_hbm, m0_hbm, basis_hbm, wig_hbm, src_hbm, dst_hbm,
    next_ref, prev_ref, meta_ref,
    lists_ref, teacher_ref, student_ref, m0_ref, basis_ref, wig_ref, src_ref, dst_ref,
    wigf_ref, rows_ref, sems,
):
    copies = fetch(
        (
            (lists_hbm, lists_ref), (teacher_hbm, teacher_ref), (student_hbm, student_ref),
            (m0_hbm.at[:, :C], m0_ref), (basis_hbm, basis_ref), (wig_hbm, wig_ref),
            (src_hbm, src_ref), (dst_hbm, dst_ref),
        ),
        sems,
    )
    for copy in copies:
        copy.wait()
    rows = lax.broadcasted_iota(jnp.int32, (OWN, 16), 0)
    for k, out_ref in enumerate((next_ref, prev_ref)):
        pick = (rows == lists_ref[0, k : k + 1, :]).astype(F32).astype(BF)
        out_ref[:, :KC] = dot(pick, teacher_ref[...], ((0,), (0,))).astype(BF)
        out_ref[:, KC:] = dot(pick, student_ref[...], ((0,), (0,))).astype(BF)
    wigf_ref[...] = wig_ref[...].astype(F32)
    rows_ref[...] = jnp.zeros_like(rows_ref)
    for degree in range(LMAX + 1):
        span = 2 * degree + 1
        row = OFFSET[degree] + min(degree, MMAX) * span
        rows_ref[degree * degree : degree * degree + span] = wigf_ref[row : row + span]
    rows_ref[49:50] = src_ref[...].astype(F32)
    rows_ref[50:51] = live_dst(dst_ref[...], count_ref[0])
    edges = rows_ref[...].astype(BF)
    for r in range(4):
        meta_ref[r, :224] = m0_ref[...]
        meta_ref[r, 224:352] = basis_ref[...]
        meta_ref[r, 352:] = edges


def live_dst(dst_row, count):
    return jnp.where(live_row(count), dst_row, EXT).astype(F32)


def pack_body(m0_hbm, m1_hbm, m2_hbm, low_ref, high_ref, m0_ref, m1_ref, m2_ref, sems):
    copies = fetch(((m0_hbm, m0_ref), (m1_hbm, m1_ref), (m2_hbm, m2_ref)), sems)
    at = 0
    for part, wide, high, ready in (
        (m0_ref, 7, 224, 0), (m1_ref.at[0], 6, 192, 1), (m1_ref.at[1], 6, 192, None),
        (m2_ref.at[0], 5, 160, 2), (m2_ref.at[1], 5, 160, None),
    ):
        if ready is not None:
            copies[ready].wait()
        for n in range(wide):
            block = part[:, n * C : (n + 1) * C]
            if at < LOW:
                low_ref[at : at + high] = block
            else:
                high_ref[at - LOW : at - LOW + high] = block
            at += high


def coefficients(refs, degree):
    parts = []
    for j in range(2 * degree + 1):
        lo = (degree * degree + j) * C
        parts += [ref[:, lo : lo + C] for ref in refs]
    return jnp.concatenate(parts, axis=0)


def gain_of(basis, radial):
    return dot(radial, basis.astype(F32).T.astype(BF), ((0,), (0,)))


def keep_turned(pack_ref, block, start, part, base):
    row = 0
    while row < C:
        which = (start + row) // part
        inside = (start + row) % part
        size = min(C - row, part - inside)
        pack_ref[which, base + inside : base + inside + size] = block[row : row + size]
        row += size


def early_body(inv_atoms, atoms_ref, rep_ref, *refs):
    raw = refs[:11]
    grad_ref = refs[11]
    held = refs[12:23]
    turn_ref, rotated_ref, hidden_ref, ssrc_ref, sdst_ref, target_ref, sems = refs[23:]
    (
        meta_ref, left_ref, right_ref, teacher_ref, student_ref, radial_ref, wsrc_ref, wdst_ref,
        wrad_ref, wout_ref, whead_ref,
    ) = held
    for copy in fetch(tuple(zip(raw, held)), sems):
        copy.wait()
    every = 4 * EDGE
    edges = [meta_ref[q, 352:416].astype(F32) for q in range(4)]
    ext_rows = lax.broadcasted_iota(jnp.int32, (EXT, EDGE), 0).astype(F32)
    sources = [(edges[q][49:50] == ext_rows).astype(F32) for q in range(4)]
    targets = [(edges[q][50:51] == ext_rows[:OWN]).astype(F32) for q in range(4)]
    gains = jnp.concatenate(
        [gain_of(meta_ref[q, 224:352], radial_ref[...]) for q in range(4)], axis=1
    )
    for degree in range(LMAX + 1):
        span = 2 * degree + 1
        for q in range(4):
            for j in range(span):
                row = degree * degree + j
                turn_ref[j * EXT : (j + 1) * EXT, q * EDGE : (q + 1) * EDGE] = (
                    sources[q] * edges[q][row : row + 1]
                ).astype(BF)
        stacked = coefficients((teacher_ref, left_ref, right_ref), degree)
        turned = dot(stacked, turn_ref[: span * EXT], ((0,), (0,)))
        rotated_ref[degree * C : (degree + 1) * C] = (turned * gains).astype(BF)
    column = jnp.concatenate([meta_ref[q, :224] for q in range(4)], axis=0)
    invariant = dot(rotated_ref[...], column, ((0,), (0,))).astype(BF)
    scatter = jnp.concatenate([targets[q] * edges[q][0:1] for q in range(4)], axis=1).astype(BF)
    invariants = dot(scatter, invariant)
    student_ext = jnp.concatenate(
        [student_ref[...], left_ref[:, KC:], right_ref[:, KC:]], axis=0
    )
    basis = jnp.concatenate([meta_ref[q, 224:352] for q in range(4)], axis=0)
    source = jnp.concatenate(sources, axis=1).astype(BF)
    onehot = jnp.concatenate(targets, axis=1).astype(BF)
    ssrc = dot(source, student_ext, ((0,), (0,))).astype(BF)
    sdst = dot(onehot, student_ref[...], ((0,), (0,))).astype(BF)
    hidden = dot(ssrc, wsrc_ref[...]) + dot(sdst, wdst_ref[...]) + dot(basis, wrad_ref[...])
    gated = (hidden * jax.nn.sigmoid(hidden)).astype(BF)
    hidden_ref[...] = hidden
    ssrc_ref[...] = ssrc
    sdst_ref[...] = sdst
    for q in range(4):
        target_ref[q] = targets[q].astype(BF)

    inv_degree = 1.0 / math.sqrt(DEG)
    target = (teacher_ref[:, :C].astype(F32) + inv_degree * invariants).astype(BF)
    pooled = (dot(onehot, gated) * inv_degree).astype(BF)
    updated = (student_ref[...].astype(F32) + dot(pooled, wout_ref[...])).astype(BF)
    predicted = dot(updated, whead_ref[...])
    rows = lax.broadcasted_iota(jnp.int32, (OWN, 1), 0)
    residual = jnp.where(rows < atoms_ref[0], predicted - target.astype(F32), 0.0)
    scaled = (residual * inv_atoms).astype(BF)
    upstream = dot(scaled, whead_ref[...], ((1,), (1,))).astype(BF)
    rep = rep_ref[0]
    mine = (rows >= rep * 8) & (rows < rep * 8 + 8)
    scaled_part = jnp.where(mine, scaled.astype(F32), 0.0).astype(BF)
    upstream_part = jnp.where(mine, upstream.astype(F32), 0.0).astype(BF)
    grad_head = dot(updated, scaled_part, ((0,), (0,)))
    grad_out = dot(pooled, upstream_part, ((0,), (0,)))
    pooled_grad = dot(upstream, wout_ref[...], ((1,), (1,))).astype(BF)
    own = pl.ds(pl.multiple_of(rep * EDGE, EDGE), EDGE)
    edge_grad = dot(target_ref[rep], pooled_grad, ((0,), (0,))) * inv_degree
    hidden = hidden_ref[own, :]
    logistic = jax.nn.sigmoid(hidden)
    hidden_grad = (edge_grad * logistic * (1.0 + hidden * (1.0 - logistic))).astype(BF)
    high = grad_ref.shape[1]
    for start, stop, value in (
        (0, 256, dot(ssrc_ref[own, :], hidden_grad, ((0,), (0,)))),
        (256, 512, dot(sdst_ref[own, :], hidden_grad, ((0,), (0,)))),
        (512, 768, grad_out),
        (768, 896, dot(meta_ref[rep, 224:352], hidden_grad, ((0,), (0,)))),
        (896, 1024, jnp.concatenate([grad_head[:C], grad_head[C:]], axis=1)),
    ):
        grad_ref[start // high : stop // high] = value.astype(BF).reshape(-1, high, SW)


def rotate_body(count_ref, rep_ref, *refs):
    raw = refs[:8]
    after_ref, keep_ref, give_ref = refs[8:11]
    held = refs[11:19]
    pack_ref, wigf_ref, turn_ref, sems = refs[19:]
    teacher_ref, left_ref, right_ref, wig_ref, basis_ref, radial_ref, src_ref, dst_ref = held
    for copy in fetch(tuple(zip(raw, held)), sems):
        copy.wait()
    rep = rep_ref[0]
    wigf_ref[:235] = wig_ref[...].astype(F32)
    wigf_ref[235:] = jnp.broadcast_to(live_dst(dst_ref[...], count_ref[0]), (5, EDGE))
    source = (src_ref[...] == lax.broadcasted_iota(jnp.int32, (EXT, EDGE), 0)).astype(F32)
    gain = gain_of(basis_ref[...], radial_ref[...])
    for degree in range(LMAX + 1):
        cap = min(degree, MMAX)
        span = 2 * degree + 1
        orders = 2 * cap + 1
        for morder in range(orders):
            for j in range(span):
                row = OFFSET[degree] + morder * span + j
                turn_ref[j * EXT : (j + 1) * EXT, morder * EDGE : (morder + 1) * EDGE] = (
                    source * wigf_ref[row : row + 1, :]
                ).astype(BF)
        stacked = coefficients((teacher_ref, left_ref, right_ref), degree)
        turned = dot(stacked, turn_ref[: span * EXT, : orders * EDGE], ((0,), (0,)))
        for morder in range(orders):
            block = (turned[:, morder * EDGE : (morder + 1) * EDGE] * gain).astype(BF)
            signed = morder - cap
            part, base = SECTIONS[signed]
            keep_turned(pack_ref, block, (degree - abs(signed)) * C, part, base)
    edges = wigf_ref[...].astype(BF)
    for out_ref, first in ((keep_ref, 0), (give_ref, 1)):
        out_ref[:928] = pack_ref[rep ^ first]
        out_ref[928:1856] = pack_ref[rep ^ (first + 2)]
        out_ref[1856:] = edges


def spread_body(parts_ref, *refs):
    out_ref = refs[-1]
    total = parts_ref[0].astype(F32)
    for i in range(1, parts_ref.shape[0]):
        total += parts_ref[i].astype(F32)
    total = total.astype(out_ref.dtype)
    for i in range(out_ref.shape[0]):
        out_ref[i] = total


def unpack_body(all_ref, src_ref, dst_ref, radial_ref, out_ref, head_ref):
    values = all_ref[...].astype(F32).reshape(1024, SW)
    src_ref[...] = values[:256]
    dst_ref[...] = values[256:512]
    out_ref[...] = values[512:768]
    radial_ref[...] = values[768:896]
    head_ref[:C] = values[896:, :C]
    head_ref[C:] = values[896:, C:]


def blocks(ref, at, count, high):
    return jnp.concatenate(
        [ref[at + n * high : at + (n + 1) * high] for n in range(count)], axis=1
    )


def mix_body(
    rep_ref, keep_ref, got_ref, low_ref, high_ref, far_low_ref, far_high_ref, after_ref,
    o0_ref, o1_ref, o2_ref, o3_ref,
    wigf_ref, back_ref, sums_ref,
):
    rep = rep_ref[0]
    groups = (keep_ref, got_ref)
    own_rows = lax.broadcasted_iota(jnp.int32, (OWN, EDGE), 0).astype(F32)
    targets = []
    for g in range(2):
        wigf_ref[g] = groups[g][1856:].astype(F32)
        targets.append((wigf_ref[g, 235:236] == own_rows).astype(F32))
    lows = (low_ref, far_low_ref)
    highs = (high_ref, far_high_ref)
    over = ((0,), (0,))

    def rows(k, base, size):
        at = 928 * k + base
        return [group[at : at + size] for group in groups]

    y0 = 0.0
    for k in range(2):
        y0 += dot(jnp.concatenate(rows(k, 0, 224), axis=1), blocks(lows[k], 0, 7, 224), over)
    y0 = y0.astype(BF)
    mixed = [None]
    both = 2 * EDGE
    for wide, base in ((6, 224), (5, 608)):
        size = wide * 32
        real = 0.0
        imag = 0.0
        for k in range(2):
            pair = jnp.concatenate(rows(k, base, size) + rows(k, base + size, size), axis=1)
            if wide == 6:
                first = blocks(lows[k], 1568, 6, 192)
                second = blocks(highs[k], 0, 6, 192)
            else:
                first = blocks(highs[k], 1152, 5, 160)
                second = blocks(highs[k], 1952, 5, 160)
            real += dot(pair, first, over)
            imag += dot(pair, second, over)
        plus = (real[:both] - imag[both:]).astype(BF)
        minus = (imag[:both] + real[both:]).astype(BF)
        mixed.append((plus, minus))
    for degree in range(LMAX + 1):
        cap = min(degree, MMAX)
        span = 2 * degree + 1
        orders = 2 * cap + 1
        stacked = []
        for morder in range(orders):
            signed = morder - cap
            if signed == 0:
                stacked.append(y0[:, degree * C : (degree + 1) * C])
            else:
                slot = degree - abs(signed)
                part = mixed[abs(signed)][0 if signed > 0 else 1]
                stacked.append(part[:, slot * C : (slot + 1) * C])
            for j in range(span):
                row = OFFSET[degree] + morder * span + j
                for g in range(2):
                    lane = morder * both + g * EDGE
                    back_ref[j * OWN : (j + 1) * OWN, lane : lane + EDGE] = (
                        targets[g] * wigf_ref[g, row : row + 1, :]
                    ).astype(BF)
        summed = dot(
            back_ref[: span * OWN, : orders * both], jnp.concatenate(stacked, axis=0)
        )
        for j in range(span):
            lo = (degree * degree + j) * C
            sums_ref[:, lo : lo + C] = summed[j * OWN : (j + 1) * OWN]
    for k, out_ref in enumerate((o0_ref, o1_ref, o2_ref, o3_ref)):
        start = pl.multiple_of((rep ^ k) * 8, 8)
        out_ref[...] = sums_ref[pl.ds(start, 8), :].astype(out_ref.dtype)


def finish_body(own_ref, s0_ref, s1_ref, s2_ref, s3_ref, out_ref):
    total = (s0_ref[...] + s1_ref[...].astype(F32)) + (
        s2_ref[...].astype(F32) + s3_ref[...].astype(F32)
    )
    out_ref[...] = (own_ref[...].astype(F32) + total * (1.0 / math.sqrt(DEG))).astype(BF)


def call(body, outs, ins, scratch=(), scalars=0, raws=0, after=0, flops=0, room=24 << 10):
    specs = [SMEM] * scalars + [VMEM] * (len(ins) - scalars - raws - after)
    return pl.pallas_call(
        body,
        out_shape=tuple(jax.ShapeDtypeStruct(shape, dtype) for shape, dtype in outs),
        in_specs=specs + [HBM] * raws + [ANY] * after,
        out_specs=tuple(VMEM for _ in outs),
        scratch_shapes=list(scratch),
        compiler_params=pltpu.CompilerParams(vmem_limit_bytes=(FULL - room) << 10),
        cost_estimate=pl.CostEstimate(flops=flops, bytes_accessed=4096, transcendentals=0),
    )(*ins)


def held(arrays):
    return [pltpu.VMEM(array.shape, array.dtype) for array in arrays]


def shifted(x, axes, by):
    length = lax.axis_size(axes)
    return lax.ppermute(x, axes, [(i, (i + by) % length) for i in range(length)])


def swapped(x, axes, mask):
    return lax.ppermute(x, axes, [(i, i ^ mask) for i in range(lax.axis_size(axes))])


def exchange(x, axes):
    return lax.all_to_all(x, axes, 0, 0, tiled=True)


def per_device(
    teacher_in, student_in, wigner, edge_basis, teacher_radial, so2_m0, so2_m1, so2_m2,
    w_src, w_dst, w_radial, w_out, w_head, src, dst, edge_count, atom_count, send_idx,
):
    bricks = lax.axis_size(BRICK)
    plane = lax.axis_size(PLANE)
    line = lax.axis_size("z")
    rep = lax.axis_index(REP).astype(jnp.int32)
    rep1 = rep.reshape(1)
    src_row = src.reshape(1, EDGE)
    dst_row = dst.reshape(1, EDGE)
    chunk = 1024 // plane
    raw = (send_idx, teacher_in, student_in, so2_m0, edge_basis, wigner, src_row, dst_row)
    to_next, to_prev, own_meta = call(
        start_body,
        [((16, KC + SW), BF), ((16, KC + SW), BF), ((4, 416, C), BF)],
        (edge_count, *raw),
        held(raw[:3])
        + [pltpu.VMEM((224, C), BF)]
        + held(raw[4:])
        + [
            pltpu.VMEM((235, EDGE), F32), pltpu.VMEM((64, EDGE), F32),
            pltpu.SemaphoreType.DMA((8,)),
        ],
        scalars=1,
        raws=8,
        room=1024,
    )
    from_left = shifted(to_next, BRICK, 1)
    from_right = shifted(to_prev, BRICK, -1)
    meta = exchange(own_meta, REP)
    mixings = (so2_m0, so2_m1, so2_m2)
    low, high = call(
        pack_body,
        [((LOW, C), BF), ((HIGH, C), BF)],
        mixings,
        held(mixings) + [pltpu.SemaphoreType.DMA((3,))],
        raws=3,
        flops=1 << 30,
        room=1024,
    )
    raw = (
        meta, from_left, from_right, teacher_in, student_in, teacher_radial, w_src, w_dst,
        w_radial, w_out, w_head,
    )
    (grads,) = call(
        functools.partial(early_body, 1.0 / (OWN * bricks)),
        [((plane, chunk, SW), BF)],
        (atom_count, rep1, *raw),
        held(raw)
        + [
            pltpu.VMEM((13 * EXT, 4 * EDGE), BF), pltpu.VMEM((896, 4 * EDGE), BF),
            pltpu.VMEM((4 * EDGE, SW), F32), pltpu.VMEM((4 * EDGE, SW), BF),
            pltpu.VMEM((4 * EDGE, SW), BF), pltpu.VMEM((4, OWN, EDGE), BF),
            pltpu.SemaphoreType.DMA((11,)),
        ],
        scalars=2,
        raws=11,
        flops=1 << 31,
        room=1024,
    )
    low, high, grads = lax.optimization_barrier((low, high, grads))
    across_low = shifted(low, ("yh", "yl"), 1)
    across_high = shifted(high, ("yh", "yl"), -1)
    plane_parts = exchange(grads, PLANE)
    raw = (
        teacher_in, from_left, from_right, wigner, edge_basis, teacher_radial, src_row, dst_row
    )
    keep, give = call(
        rotate_body,
        [((1856 + 240, EDGE), BF)] * 2,
        (edge_count, rep1, *raw, grads),
        held(raw)
        + [
            pltpu.VMEM((4, 928, EDGE), BF), pltpu.VMEM((240, EDGE), F32),
            pltpu.VMEM((13 * EXT, 5 * EDGE), BF), pltpu.SemaphoreType.DMA((8,)),
        ],
        scalars=2,
        raws=8,
        after=1,
        flops=1 << 31,
        room=4096,
    )
    got = swapped(give, "core", 1)
    plane_parts, keep = lax.optimization_barrier((plane_parts, keep))
    (plane_sum,) = call(spread_body, [((line, chunk, SW), BF)], (plane_parts,))
    shares = call(
        mix_body,
        [((8, KC), F32)] + [((8, KC), BF)] * 3,
        (rep1, keep, got, low, high, across_low, across_high, plane_sum),
        [
            pltpu.VMEM((2, 240, EDGE), F32),
            pltpu.VMEM((13 * OWN, 10 * EDGE), BF),
            pltpu.VMEM((OWN, KC), F32),
        ],
        scalars=1,
        after=1,
        flops=1 << 32,
    )
    line_parts = exchange(plane_sum, "z")
    line_parts, share = lax.optimization_barrier((line_parts, shares[0]))
    (total,) = call(spread_body, [((plane, chunk, SW), BF)], (line_parts,))
    arrived = [share] + [swapped(shares[k], REP, k) for k in (1, 2, 3)]
    totals = exchange(total, PLANE)
    arrived = [share] + [swapped(shares[k], REP, k) for k in (1, 2, 3)]
    mine = lax.dynamic_slice_in_dim(teacher_in, rep * 8, 8, 0)
    (teacher_out,) = call(finish_body, [((8, KC), BF)], (mine, *arrived))
    grads_out = call(
        unpack_body,
        [((256, SW), F32), ((256, SW), F32), ((128, SW), F32), ((256, SW), F32), ((256, C), F32)],
        (totals,),
    )
    return (teacher_out, *grads_out)


def solution(mesh):
    fine = Mesh(mesh.devices.reshape(16, 4, 2, 2, 2), BRICK + REP)
    every = BRICK + REP
    placed = (
        P(BRICK, None),
        P(BRICK, None),
        P(None, every),
        P(every, None),
        P(),
        P(REP, None),
        P(None, REP, None),
        P(None, REP, None),
        P(),
        P(),
        P(),
        P(),
        P(),
        P(every),
        P(every),
        P(every),
        P(BRICK),
        P(BRICK, None, None),
    )
    return jax.shard_map(
        per_device,
        mesh=fine,
        in_specs=placed,
        out_specs=(P(every, None), P(), P(), P(), P(), P()),
        check_vma=False,
    )
```

```python
import functools
import math

import jax
import jax.numpy as jnp
from jax import lax
from jax.experimental import pallas as pl
from jax.experimental.pallas import tpu as pltpu
from jax.sharding import Mesh, PartitionSpec as P

LMAX = 6
MMAX = 2
DEG = 16
C = 128
OWN = 32
EXT = 64
EDGE = 128
SW = 256
KC = 6272
FULL = 64 << 10
LOW = 7 * 224 + 6 * 192
HIGH = 6 * 192 + 10 * 160
SECTIONS = {0: (224, 0), 1: (192, 224), -1: (192, 416), 2: (160, 608), -2: (160, 768)}
BF = jnp.bfloat16
F32 = jnp.float32
BRICK = ("z", "x", "yh")
REP = ("yl", "core")
PLANE = ("x", "yh", "yl", "core")
VMEM = pl.BlockSpec(memory_space=pltpu.VMEM)
HBM = pl.BlockSpec(memory_space=pltpu.HBM)
ANY = pl.BlockSpec(memory_space=pl.ANY)
SMEM = pl.BlockSpec(memory_space=pltpu.SMEM)


def offsets():
    found = []
    row = 0
    for degree in range(LMAX + 1):
        found.append(row)
        row += (2 * min(degree, MMAX) + 1) * (2 * degree + 1)
    return found


OFFSET = offsets()


def dot(left, right, over=((1,), (0,))):
    return lax.dot_general(left, right, (over, ((), ())), preferred_element_type=F32)


def live_row(count):
    return lax.broadcasted_iota(jnp.int32, (1, EDGE), 1) < count


def fetch(pairs, sems):
    copies = [
        pltpu.make_async_copy(source, target, sems.at[i])
        for i, (source, target) in enumerate(pairs)
    ]
    for copy in copies:
        copy.start()
    return copies


def start_body(
    count_ref, lists_hbm, teacher_hbm, student_hbm, m0_hbm, basis_hbm, wig_hbm, src_hbm, dst_hbm,
    next_ref, prev_ref, meta_ref,
    lists_ref, teacher_ref, student_ref, m0_ref, basis_ref, wig_ref, src_ref, dst_ref,
    wigf_ref, rows_ref, sems,
):
    copies = fetch(
        (
            (lists_hbm, lists_ref), (teacher_hbm, teacher_ref), (student_hbm, student_ref),
            (m0_hbm.at[:, :C], m0_ref), (basis_hbm, basis_ref), (wig_hbm, wig_ref),
            (src_hbm, src_ref), (dst_hbm, dst_ref),
        ),
        sems,
    )
    for copy in copies:
        copy.wait()
    rows = lax.broadcasted_iota(jnp.int32, (OWN, 16), 0)
    for k, out_ref in enumerate((next_ref, prev_ref)):
        pick = (rows == lists_ref[0, k : k + 1, :]).astype(F32).astype(BF)
        out_ref[:, :KC] = dot(pick, teacher_ref[...], ((0,), (0,))).astype(BF)
        out_ref[:, KC:] = dot(pick, student_ref[...], ((0,), (0,))).astype(BF)
    wigf_ref[...] = wig_ref[...].astype(F32)
    rows_ref[...] = jnp.zeros_like(rows_ref)
    for degree in range(LMAX + 1):
        span = 2 * degree + 1
        row = OFFSET[degree] + min(degree, MMAX) * span
        rows_ref[degree * degree : degree * degree + span] = wigf_ref[row : row + span]
    rows_ref[49:50] = src_ref[...].astype(F32)
    rows_ref[50:51] = live_dst(dst_ref[...], count_ref[0])
    edges = rows_ref[...].astype(BF)
    for r in range(4):
        meta_ref[r, :224] = m0_ref[...]
        meta_ref[r, 224:352] = basis_ref[...]
        meta_ref[r, 352:] = edges


def live_dst(dst_row, count):
    return jnp.where(live_row(count), dst_row, EXT).astype(F32)


def pack_body(m0_hbm, m1_hbm, m2_hbm, low_ref, high_ref, m0_ref, m1_ref, m2_ref, sems):
    copies = fetch(((m0_hbm, m0_ref), (m1_hbm, m1_ref), (m2_hbm, m2_ref)), sems)
    at = 0
    for part, wide, high, ready in (
        (m0_ref, 7, 224, 0), (m1_ref.at[0], 6, 192, 1), (m1_ref.at[1], 6, 192, None),
        (m2_ref.at[0], 5, 160, 2), (m2_ref.at[1], 5, 160, None),
    ):
        if ready is not None:
            copies[ready].wait()
        for n in range(wide):
            block = part[:, n * C : (n + 1) * C]
            if at < LOW:
                low_ref[at : at + high] = block
            else:
                high_ref[at - LOW : at - LOW + high] = block
            at += high


def coefficients(refs, degree):
    parts = []
    for j in range(2 * degree + 1):
        lo = (degree * degree + j) * C
        parts += [ref[:, lo : lo + C] for ref in refs]
    return jnp.concatenate(parts, axis=0)


def gain_of(basis, radial):
    return dot(radial, basis.astype(F32).T.astype(BF), ((0,), (0,)))


def keep_turned(pack_ref, block, start, part, base):
    row = 0
    while row < C:
        which = (start + row) // part
        inside = (start + row) % part
        size = min(C - row, part - inside)
        pack_ref[which, base + inside : base + inside + size] = block[row : row + size]
        row += size


def early_body(inv_atoms, atoms_ref, rep_ref, meta_ref, left_ref, right_ref, *refs):
    raw = refs[:8]
    grad_ref = refs[8]
    held = refs[9:17]
    turn_ref, rotated_ref, hidden_ref, ssrc_ref, sdst_ref, target_ref, sems = refs[17:]
    (
        radial_ref, teacher_ref, student_ref, wsrc_ref, wdst_ref, wrad_ref, wout_ref, whead_ref,
    ) = held
    copies = fetch(tuple(zip(raw, held)), sems)
    every = 4 * EDGE
    edges = [meta_ref[q, 352:416].astype(F32) for q in range(4)]
    ext_rows = lax.broadcasted_iota(jnp.int32, (EXT, EDGE), 0).astype(F32)
    sources = [(edges[q][49:50] == ext_rows).astype(F32) for q in range(4)]
    targets = [(edges[q][50:51] == ext_rows[:OWN]).astype(F32) for q in range(4)]
    copies[0].wait()
    gains = jnp.concatenate(
        [gain_of(meta_ref[q, 224:352], radial_ref[...]) for q in range(4)], axis=1
    )
    for degree in range(LMAX + 1):
        span = 2 * degree + 1
        for q in range(4):
            for j in range(span):
                row = degree * degree + j
                turn_ref[j * EXT : (j + 1) * EXT, q * EDGE : (q + 1) * EDGE] = (
                    sources[q] * edges[q][row : row + 1]
                ).astype(BF)
        if degree == 0:
            copies[1].wait()
        stacked = coefficients((teacher_ref, left_ref, right_ref), degree)
        turned = dot(stacked, turn_ref[: span * EXT], ((0,), (0,)))
        rotated_ref[degree * C : (degree + 1) * C] = (turned * gains).astype(BF)
    column = jnp.concatenate([meta_ref[q, :224] for q in range(4)], axis=0)
    invariant = dot(column, rotated_ref[...], ((0,), (0,))).astype(BF)
    scatter = jnp.concatenate([targets[q] * edges[q][0:1] for q in range(4)], axis=1).astype(BF)
    invariants = dot(scatter, invariant, ((1,), (1,)))
    for copy in copies[2:]:
        copy.wait()
    student_ext = jnp.concatenate(
        [student_ref[...], left_ref[:, KC:], right_ref[:, KC:]], axis=0
    )
    basis = jnp.concatenate([meta_ref[q, 224:352] for q in range(4)], axis=0)
    source = jnp.concatenate(sources, axis=1).astype(BF)
    onehot = jnp.concatenate(targets, axis=1).astype(BF)
    ssrc = dot(source, student_ext, ((0,), (0,))).astype(BF)
    sdst = dot(onehot, student_ref[...], ((0,), (0,))).astype(BF)
    hidden = dot(ssrc, wsrc_ref[...]) + dot(sdst, wdst_ref[...]) + dot(basis, wrad_ref[...])
    gated = (hidden * jax.nn.sigmoid(hidden)).astype(BF)
    hidden_ref[...] = hidden
    ssrc_ref[...] = ssrc
    sdst_ref[...] = sdst
    for q in range(4):
        target_ref[q] = targets[q].astype(BF)

    inv_degree = 1.0 / math.sqrt(DEG)
    target = (teacher_ref[:, :C].astype(F32) + inv_degree * invariants).astype(BF)
    pooled = (dot(onehot, gated) * inv_degree).astype(BF)
    updated = (student_ref[...].astype(F32) + dot(pooled, wout_ref[...])).astype(BF)
    predicted = dot(updated, whead_ref[...])
    rows = lax.broadcasted_iota(jnp.int32, (OWN, 1), 0)
    residual = jnp.where(rows < atoms_ref[0], predicted - target.astype(F32), 0.0)
    scaled = (residual * inv_atoms).astype(BF)
    upstream = dot(scaled, whead_ref[...], ((1,), (1,))).astype(BF)
    rep = rep_ref[0]
    mine = (rows >= rep * 8) & (rows < rep * 8 + 8)
    scaled_part = jnp.where(mine, scaled.astype(F32), 0.0).astype(BF)
    upstream_part = jnp.where(mine, upstream.astype(F32), 0.0).astype(BF)
    grad_head = dot(updated, scaled_part, ((0,), (0,)))
    grad_out = dot(pooled, upstream_part, ((0,), (0,)))
    pooled_grad = dot(upstream, wout_ref[...], ((1,), (1,))).astype(BF)
    own = pl.ds(pl.multiple_of(rep * EDGE, EDGE), EDGE)
    edge_grad = dot(target_ref[rep], pooled_grad, ((0,), (0,))) * inv_degree
    hidden = hidden_ref[own, :]
    logistic = jax.nn.sigmoid(hidden)
    hidden_grad = (edge_grad * logistic * (1.0 + hidden * (1.0 - logistic))).astype(BF)
    high = grad_ref.shape[1]
    for start, stop, value in (
        (0, 256, dot(ssrc_ref[own, :], hidden_grad, ((0,), (0,)))),
        (256, 512, dot(sdst_ref[own, :], hidden_grad, ((0,), (0,)))),
        (512, 768, grad_out),
        (768, 896, dot(meta_ref[rep, 224:352], hidden_grad, ((0,), (0,)))),
        (896, 1024, jnp.concatenate([grad_head[:C], grad_head[C:]], axis=1)),
    ):
        grad_ref[start // high : stop // high] = value.astype(BF).reshape(-1, high, SW)


def rotate_body(count_ref, rep_ref, left_ref, right_ref, *refs):
    raw = refs[:6]
    after_ref, keep_ref, give_ref = refs[6:9]
    held = refs[9:15]
    pack_ref, wigf_ref, turn_ref, sems = refs[15:]
    teacher_ref, wig_ref, basis_ref, radial_ref, src_ref, dst_ref = held
    for copy in fetch(tuple(zip(raw, held)), sems):
        copy.wait()
    rep = rep_ref[0]
    wigf_ref[:235] = wig_ref[...].astype(F32)
    wigf_ref[235:] = jnp.broadcast_to(live_dst(dst_ref[...], count_ref[0]), (5, EDGE))
    source = (src_ref[...] == lax.broadcasted_iota(jnp.int32, (EXT, EDGE), 0)).astype(F32)
    gain = gain_of(basis_ref[...], radial_ref[...])
    for degree in range(LMAX + 1):
        cap = min(degree, MMAX)
        span = 2 * degree + 1
        orders = 2 * cap + 1
        for morder in range(orders):
            for j in range(span):
                row = OFFSET[degree] + morder * span + j
                turn_ref[j * EXT : (j + 1) * EXT, morder * EDGE : (morder + 1) * EDGE] = (
                    source * wigf_ref[row : row + 1, :]
                ).astype(BF)
        stacked = coefficients((teacher_ref, left_ref, right_ref), degree)
        turned = dot(stacked, turn_ref[: span * EXT, : orders * EDGE], ((0,), (0,)))
        for morder in range(orders):
            block = (turned[:, morder * EDGE : (morder + 1) * EDGE] * gain).astype(BF)
            signed = morder - cap
            part, base = SECTIONS[signed]
            keep_turned(pack_ref, block, (degree - abs(signed)) * C, part, base)
    edges = wigf_ref[...].astype(BF)
    for out_ref, first in ((keep_ref, 0), (give_ref, 1)):
        out_ref[:928] = pack_ref[rep ^ first]
        out_ref[928:1856] = pack_ref[rep ^ (first + 2)]
        out_ref[1856:] = edges


def spread_body(parts_ref, *refs):
    out_ref = refs[-1]
    total = parts_ref[0].astype(F32)
    for i in range(1, parts_ref.shape[0]):
        total += parts_ref[i].astype(F32)
    total = total.astype(out_ref.dtype)
    for i in range(out_ref.shape[0]):
        out_ref[i] = total


def unpack_body(all_ref, src_ref, dst_ref, radial_ref, out_ref, head_ref):
    values = all_ref[...].astype(F32).reshape(1024, SW)
    src_ref[...] = values[:256]
    dst_ref[...] = values[256:512]
    out_ref[...] = values[512:768]
    radial_ref[...] = values[768:896]
    head_ref[:C] = values[896:, :C]
    head_ref[C:] = values[896:, C:]


def blocks(ref, at, count, high):
    return jnp.concatenate(
        [ref[at + n * high : at + (n + 1) * high] for n in range(count)], axis=1
    )


def mix_body(
    rep_ref, keep_ref, got_ref, low_ref, high_ref, far_low_ref, far_high_ref, after_ref,
    o0_ref, o1_ref, o2_ref, o3_ref,
    wigf_ref, back_ref, sums_ref,
):
    rep = rep_ref[0]
    groups = (keep_ref, got_ref)
    own_rows = lax.broadcasted_iota(jnp.int32, (OWN, EDGE), 0).astype(F32)
    targets = []
    for g in range(2):
        wigf_ref[g] = groups[g][1856:].astype(F32)
        targets.append((wigf_ref[g, 235:236] == own_rows).astype(F32))
    lows = (low_ref, far_low_ref)
    highs = (high_ref, far_high_ref)
    over = ((0,), (0,))

    def rows(k, base, size):
        at = 928 * k + base
        return [group[at : at + size] for group in groups]

    y0 = 0.0
    for k in range(2):
        y0 += dot(jnp.concatenate(rows(k, 0, 224), axis=1), blocks(lows[k], 0, 7, 224), over)
    y0 = y0.astype(BF)
    mixed = [None]
    both = 2 * EDGE
    for wide, base in ((6, 224), (5, 608)):
        size = wide * 32
        real = 0.0
        imag = 0.0
        for k in range(2):
            pair = jnp.concatenate(rows(k, base, size) + rows(k, base + size, size), axis=1)
            if wide == 6:
                first = blocks(lows[k], 1568, 6, 192)
                second = blocks(highs[k], 0, 6, 192)
            else:
                first = blocks(highs[k], 1152, 5, 160)
                second = blocks(highs[k], 1952, 5, 160)
            real += dot(pair, first, over)
            imag += dot(pair, second, over)
        plus = (real[:both] - imag[both:]).astype(BF)
        minus = (imag[:both] + real[both:]).astype(BF)
        mixed.append((plus, minus))
    for degree in range(LMAX + 1):
        cap = min(degree, MMAX)
        span = 2 * degree + 1
        orders = 2 * cap + 1
        stacked = []
        for morder in range(orders):
            signed = morder - cap
            if signed == 0:
                stacked.append(y0[:, degree * C : (degree + 1) * C])
            else:
                slot = degree - abs(signed)
                part = mixed[abs(signed)][0 if signed > 0 else 1]
                stacked.append(part[:, slot * C : (slot + 1) * C])
            for j in range(span):
                row = OFFSET[degree] + morder * span + j
                for g in range(2):
                    lane = morder * both + g * EDGE
                    back_ref[j * OWN : (j + 1) * OWN, lane : lane + EDGE] = (
                        targets[g] * wigf_ref[g, row : row + 1, :]
                    ).astype(BF)
        summed = dot(
            back_ref[: span * OWN, : orders * both], jnp.concatenate(stacked, axis=0)
        )
        for j in range(span):
            lo = (degree * degree + j) * C
            sums_ref[:, lo : lo + C] = summed[j * OWN : (j + 1) * OWN]
    for k, out_ref in enumerate((o0_ref, o1_ref, o2_ref, o3_ref)):
        start = pl.multiple_of((rep ^ k) * 8, 8)
        out_ref[...] = sums_ref[pl.ds(start, 8), :].astype(out_ref.dtype)


def finish_body(own_ref, s0_ref, s1_ref, s2_ref, s3_ref, out_ref):
    total = (s0_ref[...] + s1_ref[...].astype(F32)) + (
        s2_ref[...].astype(F32) + s3_ref[...].astype(F32)
    )
    out_ref[...] = (own_ref[...].astype(F32) + total * (1.0 / math.sqrt(DEG))).astype(BF)


def call(body, outs, ins, scratch=(), scalars=0, raws=0, after=0, flops=0, room=24 << 10):
    specs = [SMEM] * scalars + [VMEM] * (len(ins) - scalars - raws - after)
    return pl.pallas_call(
        body,
        out_shape=tuple(jax.ShapeDtypeStruct(shape, dtype) for shape, dtype in outs),
        in_specs=specs + [HBM] * raws + [ANY] * after,
        out_specs=tuple(VMEM for _ in outs),
        scratch_shapes=list(scratch),
        compiler_params=pltpu.CompilerParams(vmem_limit_bytes=(FULL - room) << 10),
        cost_estimate=pl.CostEstimate(flops=flops, bytes_accessed=4096, transcendentals=0),
    )(*ins)


def held(arrays):
    return [pltpu.VMEM(array.shape, array.dtype) for array in arrays]


def shifted(x, axes, by):
    length = lax.axis_size(axes)
    return lax.ppermute(x, axes, [(i, (i + by) % length) for i in range(length)])


def swapped(x, axes, mask):
    return lax.ppermute(x, axes, [(i, i ^ mask) for i in range(lax.axis_size(axes))])


def exchange(x, axes):
    return lax.all_to_all(x, axes, 0, 0, tiled=True)


def per_device(
    teacher_in, student_in, wigner, edge_basis, teacher_radial, so2_m0, so2_m1, so2_m2,
    w_src, w_dst, w_radial, w_out, w_head, src, dst, edge_count, atom_count, send_idx,
):
    bricks = lax.axis_size(BRICK)
    plane = lax.axis_size(PLANE)
    line = lax.axis_size("z")
    rep = lax.axis_index(REP).astype(jnp.int32)
    rep1 = rep.reshape(1)
    src_row = src.reshape(1, EDGE)
    dst_row = dst.reshape(1, EDGE)
    chunk = 1024 // plane
    raw = (send_idx, teacher_in, student_in, so2_m0, edge_basis, wigner, src_row, dst_row)
    to_next, to_prev, own_meta = call(
        start_body,
        [((16, KC + SW), BF), ((16, KC + SW), BF), ((4, 416, C), BF)],
        (edge_count, *raw),
        held(raw[:3])
        + [pltpu.VMEM((224, C), BF)]
        + held(raw[4:])
        + [
            pltpu.VMEM((235, EDGE), F32), pltpu.VMEM((64, EDGE), F32),
            pltpu.SemaphoreType.DMA((8,)),
        ],
        scalars=1,
        raws=8,
        room=1024,
    )
    from_left = shifted(to_next, BRICK, 1)
    from_right = shifted(to_prev, BRICK, -1)
    meta = exchange(own_meta, REP)
    mixings = (so2_m0, so2_m1, so2_m2)
    low, high = call(
        pack_body,
        [((LOW, C), BF), ((HIGH, C), BF)],
        mixings,
        held(mixings) + [pltpu.SemaphoreType.DMA((3,))],
        raws=3,
        flops=1 << 30,
        room=1024,
    )
    raw = (
        teacher_radial, teacher_in, student_in, w_src, w_dst, w_radial, w_out, w_head
    )
    (grads,) = call(
        functools.partial(early_body, 1.0 / (OWN * bricks)),
        [((plane, chunk, SW), BF)],
        (atom_count, rep1, meta, from_left, from_right, *raw),
        held(raw)
        + [
            pltpu.VMEM((13 * EXT, 4 * EDGE), BF), pltpu.VMEM((896, 4 * EDGE), BF),
            pltpu.VMEM((4 * EDGE, SW), F32), pltpu.VMEM((4 * EDGE, SW), BF),
            pltpu.VMEM((4 * EDGE, SW), BF), pltpu.VMEM((4, OWN, EDGE), BF),
            pltpu.SemaphoreType.DMA((8,)),
        ],
        scalars=2,
        raws=8,
        flops=1 << 31,
        room=2048,
    )
    low, high, grads = lax.optimization_barrier((low, high, grads))
    across_low = shifted(low, ("yh", "yl"), 1)
    across_high = shifted(high, ("yh", "yl"), -1)
    plane_parts = exchange(grads, PLANE)
    raw = (teacher_in, wigner, edge_basis, teacher_radial, src_row, dst_row)
    keep, give = call(
        rotate_body,
        [((1856 + 240, EDGE), BF)] * 2,
        (edge_count, rep1, from_left, from_right, *raw, grads),
        held(raw)
        + [
            pltpu.VMEM((4, 928, EDGE), BF), pltpu.VMEM((240, EDGE), F32),
            pltpu.VMEM((13 * EXT, 5 * EDGE), BF), pltpu.SemaphoreType.DMA((6,)),
        ],
        scalars=2,
        raws=6,
        after=1,
        flops=1 << 31,
        room=4096,
    )
    got = swapped(give, "core", 1)
    plane_parts, keep = lax.optimization_barrier((plane_parts, keep))
    (plane_sum,) = call(spread_body, [((line, chunk, SW), BF)], (plane_parts,))
    shares = call(
        mix_body,
        [((8, KC), F32)] + [((8, KC), BF)] * 3,
        (rep1, keep, got, low, high, across_low, across_high, plane_sum),
        [
            pltpu.VMEM((2, 240, EDGE), F32),
            pltpu.VMEM((13 * OWN, 10 * EDGE), BF),
            pltpu.VMEM((OWN, KC), F32),
        ],
        scalars=1,
        after=1,
        flops=1 << 32,
    )
    line_parts = exchange(plane_sum, "z")
    line_parts, share = lax.optimization_barrier((line_parts, shares[0]))
    (total,) = call(spread_body, [((plane, chunk, SW), BF)], (line_parts,))
    total, *rest = lax.optimization_barrier((total, *shares[1:]))
    arrived = [share] + [swapped(rest[k - 1], REP, k) for k in (1, 2, 3)]
    totals = exchange(total, PLANE)
    total, *rest = lax.optimization_barrier((total, *shares[1:]))
    arrived = [share] + [swapped(rest[k - 1], REP, k) for k in (1, 2, 3)]
    mine = lax.dynamic_slice_in_dim(teacher_in, rep * 8, 8, 0)
    (teacher_out,) = call(finish_body, [((8, KC), BF)], (mine, *arrived))
    grads_out = call(
        unpack_body,
        [((256, SW), F32), ((256, SW), F32), ((128, SW), F32), ((256, SW), F32), ((256, C), F32)],
        (totals,),
    )
    return (teacher_out, *grads_out)


def solution(mesh):
    fine = Mesh(mesh.devices.reshape(16, 4, 2, 2, 2), BRICK + REP)
    every = BRICK + REP
    placed = (
        P(BRICK, None),
        P(BRICK, None),
        P(None, every),
        P(every, None),
        P(),
        P(REP, None),
        P(None, REP, None),
        P(None, REP, None),
        P(),
        P(),
        P(),
        P(),
        P(),
        P(every),
        P(every),
        P(every),
        P(BRICK),
        P(BRICK, None, None),
    )
    return jax.shard_map(
        per_device,
        mesh=fine,
        in_specs=placed,
        out_specs=(P(every, None), P(), P(), P(), P(), P()),
        check_vma=False,
    )
```

```python
import functools
import math

import jax
import jax.numpy as jnp
from jax import lax
from jax.experimental import pallas as pl
from jax.experimental.pallas import tpu as pltpu
from jax.sharding import Mesh, PartitionSpec as P

LMAX = 6
MMAX = 2
DEG = 16
C = 128
OWN = 32
EXT = 64
EDGE = 128
SW = 256
KC = 6272
FULL = 64 << 10
LOW = 7 * 224 + 6 * 192
HIGH = 6 * 192 + 10 * 160
SECTIONS = {0: (224, 0), 1: (192, 224), -1: (192, 416), 2: (160, 608), -2: (160, 768)}
BF = jnp.bfloat16
F32 = jnp.float32
BRICK = ("z", "x", "yh")
REP = ("yl", "core")
PLANE = ("x", "yh", "yl", "core")
VMEM = pl.BlockSpec(memory_space=pltpu.VMEM)
HBM = pl.BlockSpec(memory_space=pltpu.HBM)
ANY = pl.BlockSpec(memory_space=pl.ANY)
SMEM = pl.BlockSpec(memory_space=pltpu.SMEM)


def offsets():
    found = []
    row = 0
    for degree in range(LMAX + 1):
        found.append(row)
        row += (2 * min(degree, MMAX) + 1) * (2 * degree + 1)
    return found


OFFSET = offsets()


def dot(left, right, over=((1,), (0,))):
    return lax.dot_general(left, right, (over, ((), ())), preferred_element_type=F32)


def live_row(count):
    return lax.broadcasted_iota(jnp.int32, (1, EDGE), 1) < count


def fetch(pairs, sems):
    copies = [
        pltpu.make_async_copy(source, target, sems.at[i])
        for i, (source, target) in enumerate(pairs)
    ]
    for copy in copies:
        copy.start()
    return copies


def start_body(
    count_ref, lists_hbm, teacher_hbm, student_hbm, m0_hbm, basis_hbm, wig_hbm, src_hbm, dst_hbm,
    next_ref, prev_ref, meta_ref,
    lists_ref, teacher_ref, student_ref, m0_ref, basis_ref, wig_ref, src_ref, dst_ref,
    wigf_ref, rows_ref, sems,
):
    copies = fetch(
        (
            (lists_hbm, lists_ref), (teacher_hbm, teacher_ref), (student_hbm, student_ref),
            (m0_hbm.at[:, :C], m0_ref), (basis_hbm, basis_ref), (wig_hbm, wig_ref),
            (src_hbm, src_ref), (dst_hbm, dst_ref),
        ),
        sems,
    )
    for copy in copies:
        copy.wait()
    rows = lax.broadcasted_iota(jnp.int32, (OWN, 16), 0)
    for k, out_ref in enumerate((next_ref, prev_ref)):
        pick = (rows == lists_ref[0, k : k + 1, :]).astype(F32).astype(BF)
        out_ref[:, :KC] = dot(pick, teacher_ref[...], ((0,), (0,))).astype(BF)
        out_ref[:, KC:] = dot(pick, student_ref[...], ((0,), (0,))).astype(BF)
    wigf_ref[...] = wig_ref[...].astype(F32)
    rows_ref[...] = jnp.zeros_like(rows_ref)
    for degree in range(LMAX + 1):
        span = 2 * degree + 1
        row = OFFSET[degree] + min(degree, MMAX) * span
        rows_ref[degree * degree : degree * degree + span] = wigf_ref[row : row + span]
    rows_ref[49:50] = src_ref[...].astype(F32)
    rows_ref[50:51] = live_dst(dst_ref[...], count_ref[0])
    edges = rows_ref[...].astype(BF)
    for r in range(4):
        meta_ref[r, :224] = m0_ref[...]
        meta_ref[r, 224:352] = basis_ref[...]
        meta_ref[r, 352:] = edges


def live_dst(dst_row, count):
    return jnp.where(live_row(count), dst_row, EXT).astype(F32)


def pack_body(m0_hbm, m1_hbm, m2_hbm, low_ref, high_ref, m0_ref, m1_ref, m2_ref, sems):
    copies = fetch(((m0_hbm, m0_ref), (m1_hbm, m1_ref), (m2_hbm, m2_ref)), sems)
    at = 0
    for part, wide, high, ready in (
        (m0_ref, 7, 224, 0), (m1_ref.at[0], 6, 192, 1), (m1_ref.at[1], 6, 192, None),
        (m2_ref.at[0], 5, 160, 2), (m2_ref.at[1], 5, 160, None),
    ):
        if ready is not None:
            copies[ready].wait()
        for n in range(wide):
            block = part[:, n * C : (n + 1) * C]
            if at < LOW:
                low_ref[at : at + high] = block
            else:
                high_ref[at - LOW : at - LOW + high] = block
            at += high


def coefficients(refs, degree):
    parts = []
    for j in range(2 * degree + 1):
        lo = (degree * degree + j) * C
        parts += [ref[:, lo : lo + C] for ref in refs]
    return jnp.concatenate(parts, axis=0)


def gain_of(basis, radial):
    return dot(radial, basis.astype(F32).T.astype(BF), ((0,), (0,)))


def keep_turned(pack_ref, block, start, part, base):
    row = 0
    while row < C:
        which = (start + row) // part
        inside = (start + row) % part
        size = min(C - row, part - inside)
        pack_ref[which, base + inside : base + inside + size] = block[row : row + size]
        row += size


def early_body(inv_atoms, atoms_ref, rep_ref, *refs):
    raw = refs[:11]
    grad_ref = refs[11]
    held = refs[12:23]
    turn_ref, rotated_ref, hidden_ref, ssrc_ref, sdst_ref, target_ref, sems = refs[23:]
    (
        meta_ref, radial_ref, teacher_ref, left_ref, right_ref, student_ref, wsrc_ref, wdst_ref,
        wrad_ref, wout_ref, whead_ref,
    ) = held
    copies = fetch(tuple(zip(raw, held)), sems)
    for copy in copies[:2]:
        copy.wait()
    every = 4 * EDGE
    edges = [meta_ref[q, 352:416].astype(F32) for q in range(4)]
    ext_rows = lax.broadcasted_iota(jnp.int32, (EXT, EDGE), 0).astype(F32)
    sources = [(edges[q][49:50] == ext_rows).astype(F32) for q in range(4)]
    targets = [(edges[q][50:51] == ext_rows[:OWN]).astype(F32) for q in range(4)]
    gains = jnp.concatenate(
        [gain_of(meta_ref[q, 224:352], radial_ref[...]) for q in range(4)], axis=1
    )
    for degree in range(LMAX + 1):
        span = 2 * degree + 1
        for q in range(4):
            for j in range(span):
                row = degree * degree + j
                turn_ref[j * EXT : (j + 1) * EXT, q * EDGE : (q + 1) * EDGE] = (
                    sources[q] * edges[q][row : row + 1]
                ).astype(BF)
        if degree == 0:
            for copy in copies[2:]:
                copy.wait()
        stacked = coefficients((teacher_ref, left_ref, right_ref), degree)
        turned = dot(stacked, turn_ref[: span * EXT], ((0,), (0,)))
        rotated_ref[degree * C : (degree + 1) * C] = (turned * gains).astype(BF)
    column = jnp.concatenate([meta_ref[q, :224] for q in range(4)], axis=0)
    invariant = dot(column, rotated_ref[...], ((0,), (0,))).astype(BF)
    scatter = jnp.concatenate([targets[q] * edges[q][0:1] for q in range(4)], axis=1).astype(BF)
    invariants = dot(scatter, invariant, ((1,), (1,)))
    student_ext = jnp.concatenate(
        [student_ref[...], left_ref[:, KC:], right_ref[:, KC:]], axis=0
    )
    basis = jnp.concatenate([meta_ref[q, 224:352] for q in range(4)], axis=0)
    source = jnp.concatenate(sources, axis=1).astype(BF)
    onehot = jnp.concatenate(targets, axis=1).astype(BF)
    ssrc = dot(source, student_ext, ((0,), (0,))).astype(BF)
    sdst = dot(onehot, student_ref[...], ((0,), (0,))).astype(BF)
    hidden = dot(ssrc, wsrc_ref[...]) + dot(sdst, wdst_ref[...]) + dot(basis, wrad_ref[...])
    gated = (hidden * jax.nn.sigmoid(hidden)).astype(BF)
    hidden_ref[...] = hidden
    ssrc_ref[...] = ssrc
    sdst_ref[...] = sdst
    for q in range(4):
        target_ref[q] = targets[q].astype(BF)

    inv_degree = 1.0 / math.sqrt(DEG)
    target = (teacher_ref[:, :C].astype(F32) + inv_degree * invariants).astype(BF)
    pooled = (dot(onehot, gated) * inv_degree).astype(BF)
    updated = (student_ref[...].astype(F32) + dot(pooled, wout_ref[...])).astype(BF)
    predicted = dot(updated, whead_ref[...])
    rows = lax.broadcasted_iota(jnp.int32, (OWN, 1), 0)
    residual = jnp.where(rows < atoms_ref[0], predicted - target.astype(F32), 0.0)
    scaled = (residual * inv_atoms).astype(BF)
    upstream = dot(scaled, whead_ref[...], ((1,), (1,))).astype(BF)
    rep = rep_ref[0]
    mine = (rows >= rep * 8) & (rows < rep * 8 + 8)
    scaled_part = jnp.where(mine, scaled.astype(F32), 0.0).astype(BF)
    upstream_part = jnp.where(mine, upstream.astype(F32), 0.0).astype(BF)
    grad_head = dot(updated, scaled_part, ((0,), (0,)))
    grad_out = dot(pooled, upstream_part, ((0,), (0,)))
    pooled_grad = dot(upstream, wout_ref[...], ((1,), (1,))).astype(BF)
    own = pl.ds(pl.multiple_of(rep * EDGE, EDGE), EDGE)
    edge_grad = dot(target_ref[rep], pooled_grad, ((0,), (0,))) * inv_degree
    hidden = hidden_ref[own, :]
    logistic = jax.nn.sigmoid(hidden)
    hidden_grad = (edge_grad * logistic * (1.0 + hidden * (1.0 - logistic))).astype(BF)
    high = grad_ref.shape[1]
    for start, stop, value in (
        (0, 256, dot(ssrc_ref[own, :], hidden_grad, ((0,), (0,)))),
        (256, 512, dot(sdst_ref[own, :], hidden_grad, ((0,), (0,)))),
        (512, 768, grad_out),
        (768, 896, dot(meta_ref[rep, 224:352], hidden_grad, ((0,), (0,)))),
        (896, 1024, jnp.concatenate([grad_head[:C], grad_head[C:]], axis=1)),
    ):
        grad_ref[start // high : stop // high] = value.astype(BF).reshape(-1, high, SW)


def rotate_body(count_ref, rep_ref, *refs):
    raw = refs[:8]
    after_ref, keep_ref, give_ref = refs[8:11]
    held = refs[11:19]
    pack_ref, wigf_ref, turn_ref, sems = refs[19:]
    teacher_ref, left_ref, right_ref, wig_ref, basis_ref, radial_ref, src_ref, dst_ref = held
    for copy in fetch(tuple(zip(raw, held)), sems):
        copy.wait()
    rep = rep_ref[0]
    wigf_ref[:235] = wig_ref[...].astype(F32)
    wigf_ref[235:] = jnp.broadcast_to(live_dst(dst_ref[...], count_ref[0]), (5, EDGE))
    source = (src_ref[...] == lax.broadcasted_iota(jnp.int32, (EXT, EDGE), 0)).astype(F32)
    gain = gain_of(basis_ref[...], radial_ref[...])
    for degree in range(LMAX + 1):
        cap = min(degree, MMAX)
        span = 2 * degree + 1
        orders = 2 * cap + 1
        for morder in range(orders):
            for j in range(span):
                row = OFFSET[degree] + morder * span + j
                turn_ref[j * EXT : (j + 1) * EXT, morder * EDGE : (morder + 1) * EDGE] = (
                    source * wigf_ref[row : row + 1, :]
                ).astype(BF)
        stacked = coefficients((teacher_ref, left_ref, right_ref), degree)
        turned = dot(stacked, turn_ref[: span * EXT, : orders * EDGE], ((0,), (0,)))
        for morder in range(orders):
            block = (turned[:, morder * EDGE : (morder + 1) * EDGE] * gain).astype(BF)
            signed = morder - cap
            part, base = SECTIONS[signed]
            keep_turned(pack_ref, block, (degree - abs(signed)) * C, part, base)
    edges = wigf_ref[...].astype(BF)
    for out_ref, first in ((keep_ref, 0), (give_ref, 1)):
        out_ref[:928] = pack_ref[rep ^ first]
        out_ref[928:1856] = pack_ref[rep ^ (first + 2)]
        out_ref[1856:] = edges


def spread_body(parts_ref, *refs):
    out_ref = refs[-1]
    total = parts_ref[0].astype(F32)
    for i in range(1, parts_ref.shape[0]):
        total += parts_ref[i].astype(F32)
    total = total.astype(out_ref.dtype)
    for i in range(out_ref.shape[0]):
        out_ref[i] = total


def unpack_body(all_ref, src_ref, dst_ref, radial_ref, out_ref, head_ref):
    values = all_ref[...].astype(F32).reshape(1024, SW)
    src_ref[...] = values[:256]
    dst_ref[...] = values[256:512]
    out_ref[...] = values[512:768]
    radial_ref[...] = values[768:896]
    head_ref[:C] = values[896:, :C]
    head_ref[C:] = values[896:, C:]


def blocks(ref, at, count, high):
    return jnp.concatenate(
        [ref[at + n * high : at + (n + 1) * high] for n in range(count)], axis=1
    )


def mix_body(
    rep_ref, keep_ref, got_ref, low_ref, high_ref, far_low_ref, far_high_ref, after_ref,
    o0_ref, o1_ref, o2_ref, o3_ref,
    wigf_ref, back_ref, sums_ref,
):
    rep = rep_ref[0]
    groups = (keep_ref, got_ref)
    own_rows = lax.broadcasted_iota(jnp.int32, (OWN, EDGE), 0).astype(F32)
    targets = []
    for g in range(2):
        wigf_ref[g] = groups[g][1856:].astype(F32)
        targets.append((wigf_ref[g, 235:236] == own_rows).astype(F32))
    lows = (low_ref, far_low_ref)
    highs = (high_ref, far_high_ref)
    over = ((0,), (0,))

    def rows(k, base, size):
        at = 928 * k + base
        return [group[at : at + size] for group in groups]

    y0 = 0.0
    for k in range(2):
        y0 += dot(jnp.concatenate(rows(k, 0, 224), axis=1), blocks(lows[k], 0, 7, 224), over)
    y0 = y0.astype(BF)
    mixed = [None]
    both = 2 * EDGE
    for wide, base in ((6, 224), (5, 608)):
        size = wide * 32
        real = 0.0
        imag = 0.0
        for k in range(2):
            pair = jnp.concatenate(rows(k, base, size) + rows(k, base + size, size), axis=1)
            if wide == 6:
                first = blocks(lows[k], 1568, 6, 192)
                second = blocks(highs[k], 0, 6, 192)
            else:
                first = blocks(highs[k], 1152, 5, 160)
                second = blocks(highs[k], 1952, 5, 160)
            real += dot(pair, first, over)
            imag += dot(pair, second, over)
        plus = (real[:both] - imag[both:]).astype(BF)
        minus = (imag[:both] + real[both:]).astype(BF)
        mixed.append((plus, minus))
    for degree in range(LMAX + 1):
        cap = min(degree, MMAX)
        span = 2 * degree + 1
        orders = 2 * cap + 1
        stacked = []
        for morder in range(orders):
            signed = morder - cap
            if signed == 0:
                stacked.append(y0[:, degree * C : (degree + 1) * C])
            else:
                slot = degree - abs(signed)
                part = mixed[abs(signed)][0 if signed > 0 else 1]
                stacked.append(part[:, slot * C : (slot + 1) * C])
            for j in range(span):
                row = OFFSET[degree] + morder * span + j
                for g in range(2):
                    lane = morder * both + g * EDGE
                    back_ref[j * OWN : (j + 1) * OWN, lane : lane + EDGE] = (
                        targets[g] * wigf_ref[g, row : row + 1, :]
                    ).astype(BF)
        summed = dot(
            back_ref[: span * OWN, : orders * both], jnp.concatenate(stacked, axis=0)
        )
        for j in range(span):
            lo = (degree * degree + j) * C
            sums_ref[:, lo : lo + C] = summed[j * OWN : (j + 1) * OWN]
    for k, out_ref in enumerate((o0_ref, o1_ref, o2_ref, o3_ref)):
        start = pl.multiple_of((rep ^ k) * 8, 8)
        out_ref[...] = sums_ref[pl.ds(start, 8), :].astype(out_ref.dtype)


def finish_body(own_ref, s0_ref, s1_ref, s2_ref, s3_ref, out_ref):
    total = (s0_ref[...] + s1_ref[...].astype(F32)) + (
        s2_ref[...].astype(F32) + s3_ref[...].astype(F32)
    )
    out_ref[...] = (own_ref[...].astype(F32) + total * (1.0 / math.sqrt(DEG))).astype(BF)


def call(body, outs, ins, scratch=(), scalars=0, raws=0, after=0, flops=0, room=24 << 10):
    specs = [SMEM] * scalars + [VMEM] * (len(ins) - scalars - raws - after)
    return pl.pallas_call(
        body,
        out_shape=tuple(jax.ShapeDtypeStruct(shape, dtype) for shape, dtype in outs),
        in_specs=specs + [HBM] * raws + [ANY] * after,
        out_specs=tuple(VMEM for _ in outs),
        scratch_shapes=list(scratch),
        compiler_params=pltpu.CompilerParams(vmem_limit_bytes=(FULL - room) << 10),
        cost_estimate=pl.CostEstimate(flops=flops, bytes_accessed=4096, transcendentals=0),
    )(*ins)


def held(arrays):
    return [pltpu.VMEM(array.shape, array.dtype) for array in arrays]


def shifted(x, axes, by):
    length = lax.axis_size(axes)
    return lax.ppermute(x, axes, [(i, (i + by) % length) for i in range(length)])


def to_brick(x, by):
    reps = lax.axis_size(REP)
    length = lax.axis_size(BRICK) * reps
    half = reps // 2
    pairs = [(i, (i + by * reps) % length // reps * reps + (i + half) % reps) for i in range(length)]
    return lax.ppermute(x, BRICK + REP, pairs)


def swapped(x, axes, mask):
    return lax.ppermute(x, axes, [(i, i ^ mask) for i in range(lax.axis_size(axes))])


def exchange(x, axes):
    return lax.all_to_all(x, axes, 0, 0, tiled=True)


def per_device(
    teacher_in, student_in, wigner, edge_basis, teacher_radial, so2_m0, so2_m1, so2_m2,
    w_src, w_dst, w_radial, w_out, w_head, src, dst, edge_count, atom_count, send_idx,
):
    bricks = lax.axis_size(BRICK)
    plane = lax.axis_size(PLANE)
    line = lax.axis_size("z")
    rep = lax.axis_index(REP).astype(jnp.int32)
    rep1 = rep.reshape(1)
    src_row = src.reshape(1, EDGE)
    dst_row = dst.reshape(1, EDGE)
    chunk = 1024 // plane
    raw = (send_idx, teacher_in, student_in, so2_m0, edge_basis, wigner, src_row, dst_row)
    to_next, to_prev, own_meta = call(
        start_body,
        [((16, KC + SW), BF), ((16, KC + SW), BF), ((4, 416, C), BF)],
        (edge_count, *raw),
        held(raw[:3])
        + [pltpu.VMEM((224, C), BF)]
        + held(raw[4:])
        + [
            pltpu.VMEM((235, EDGE), F32), pltpu.VMEM((64, EDGE), F32),
            pltpu.SemaphoreType.DMA((8,)),
        ],
        scalars=1,
        raws=8,
        room=1024,
    )
    from_left = to_brick(to_next, 1)
    from_right = to_brick(to_prev, -1)
    meta = exchange(own_meta, REP)
    mixings = (so2_m0, so2_m1, so2_m2)
    low, high = call(
        pack_body,
        [((LOW, C), BF), ((HIGH, C), BF)],
        mixings,
        held(mixings) + [pltpu.SemaphoreType.DMA((3,))],
        raws=3,
        flops=1 << 30,
        room=1024,
    )
    raw = (
        meta, teacher_radial, teacher_in, from_left, from_right, student_in, w_src, w_dst,
        w_radial, w_out, w_head,
    )
    (grads,) = call(
        functools.partial(early_body, 1.0 / (OWN * bricks)),
        [((plane, chunk, SW), BF)],
        (atom_count, rep1, *raw),
        held(raw)
        + [
            pltpu.VMEM((13 * EXT, 4 * EDGE), BF), pltpu.VMEM((896, 4 * EDGE), BF),
            pltpu.VMEM((4 * EDGE, SW), F32), pltpu.VMEM((4 * EDGE, SW), BF),
            pltpu.VMEM((4 * EDGE, SW), BF), pltpu.VMEM((4, OWN, EDGE), BF),
            pltpu.SemaphoreType.DMA((11,)),
        ],
        scalars=2,
        raws=11,
        flops=1 << 31,
        room=1024,
    )
    low, high, grads = lax.optimization_barrier((low, high, grads))
    across_low = shifted(low, ("yh", "yl"), 1)
    across_high = shifted(high, ("yh", "yl"), -1)
    plane_parts = exchange(grads, PLANE)
    raw = (
        teacher_in, from_left, from_right, wigner, edge_basis, teacher_radial, src_row, dst_row
    )
    keep, give = call(
        rotate_body,
        [((1856 + 240, EDGE), BF)] * 2,
        (edge_count, rep1, *raw, grads),
        held(raw)
        + [
            pltpu.VMEM((4, 928, EDGE), BF), pltpu.VMEM((240, EDGE), F32),
            pltpu.VMEM((13 * EXT, 5 * EDGE), BF), pltpu.SemaphoreType.DMA((8,)),
        ],
        scalars=2,
        raws=8,
        after=1,
        flops=1 << 31,
        room=4096,
    )
    got = swapped(give, "core", 1)
    plane_parts, keep = lax.optimization_barrier((plane_parts, keep))
    (plane_sum,) = call(spread_body, [((line, chunk, SW), BF)], (plane_parts,))
    shares = call(
        mix_body,
        [((8, KC), F32)] + [((8, KC), BF)] * 3,
        (rep1, keep, got, low, high, across_low, across_high, plane_sum),
        [
            pltpu.VMEM((2, 240, EDGE), F32),
            pltpu.VMEM((13 * OWN, 10 * EDGE), BF),
            pltpu.VMEM((OWN, KC), F32),
        ],
        scalars=1,
        after=1,
        flops=1 << 32,
    )
    line_parts = exchange(plane_sum, "z")
    line_parts, share = lax.optimization_barrier((line_parts, shares[0]))
    (total,) = call(spread_body, [((plane, chunk, SW), BF)], (line_parts,))
    arrived = [share] + [swapped(shares[k], REP, k) for k in (1, 2, 3)]
    totals = exchange(total, PLANE)
    arrived = [share] + [swapped(shares[k], REP, k) for k in (1, 2, 3)]
    mine = lax.dynamic_slice_in_dim(teacher_in, rep * 8, 8, 0)
    (teacher_out,) = call(finish_body, [((8, KC), BF)], (mine, *arrived))
    grads_out = call(
        unpack_body,
        [((256, SW), F32), ((256, SW), F32), ((128, SW), F32), ((256, SW), F32), ((256, C), F32)],
        (totals,),
    )
    return (teacher_out, *grads_out)


def solution(mesh):
    fine = Mesh(mesh.devices.reshape(16, 4, 2, 2, 2), BRICK + REP)
    every = BRICK + REP
    placed = (
        P(BRICK, None),
        P(BRICK, None),
        P(None, every),
        P(every, None),
        P(),
        P(REP, None),
        P(None, REP, None),
        P(None, REP, None),
        P(),
        P(),
        P(),
        P(),
        P(),
        P(every),
        P(every),
        P(every),
        P(BRICK),
        P(BRICK, None, None),
    )
    return jax.shard_map(
        per_device,
        mesh=fine,
        in_specs=placed,
        out_specs=(P(every, None), P(), P(), P(), P(), P()),
        check_vma=False,
    )
```

```python
import functools
import math

import jax
import jax.numpy as jnp
from jax import lax
from jax.experimental import pallas as pl
from jax.experimental.pallas import tpu as pltpu
from jax.sharding import Mesh, PartitionSpec as P

LMAX = 6
MMAX = 2
DEG = 16
C = 128
OWN = 32
EXT = 64
EDGE = 128
SW = 256
KC = 6272
FULL = 64 << 10
LOW = 7 * 224 + 6 * 192
HIGH = 6 * 192 + 10 * 160
SECTIONS = {0: (224, 0), 1: (192, 224), -1: (192, 416), 2: (160, 608), -2: (160, 768)}
BF = jnp.bfloat16
F32 = jnp.float32
BRICK = ("z", "x", "yh")
REP = ("yl", "core")
PLANE = ("x", "yh", "yl", "core")
VMEM = pl.BlockSpec(memory_space=pltpu.VMEM)
HBM = pl.BlockSpec(memory_space=pltpu.HBM)
ANY = pl.BlockSpec(memory_space=pl.ANY)
SMEM = pl.BlockSpec(memory_space=pltpu.SMEM)


def offsets():
    found = []
    row = 0
    for degree in range(LMAX + 1):
        found.append(row)
        row += (2 * min(degree, MMAX) + 1) * (2 * degree + 1)
    return found


OFFSET = offsets()


def dot(left, right, over=((1,), (0,))):
    return lax.dot_general(left, right, (over, ((), ())), preferred_element_type=F32)


def live_row(count):
    return lax.broadcasted_iota(jnp.int32, (1, EDGE), 1) < count


def fetch(pairs, sems):
    copies = [
        pltpu.make_async_copy(source, target, sems.at[i])
        for i, (source, target) in enumerate(pairs)
    ]
    for copy in copies:
        copy.start()
    return copies


def start_body(
    count_ref, lists_hbm, teacher_hbm, student_hbm, m0_hbm, basis_hbm, wig_hbm, src_hbm, dst_hbm,
    next_ref, prev_ref, meta_ref,
    lists_ref, teacher_ref, student_ref, m0_ref, basis_ref, wig_ref, src_ref, dst_ref,
    wigf_ref, rows_ref, sems,
):
    copies = fetch(
        (
            (lists_hbm, lists_ref), (teacher_hbm, teacher_ref), (student_hbm, student_ref),
            (m0_hbm.at[:, :C], m0_ref), (basis_hbm, basis_ref), (wig_hbm, wig_ref),
            (src_hbm, src_ref), (dst_hbm, dst_ref),
        ),
        sems,
    )
    for copy in copies:
        copy.wait()
    rows = lax.broadcasted_iota(jnp.int32, (OWN, 16), 0)
    for k, out_ref in enumerate((next_ref, prev_ref)):
        pick = (rows == lists_ref[0, k : k + 1, :]).astype(F32).astype(BF)
        out_ref[:, :KC] = dot(pick, teacher_ref[...], ((0,), (0,))).astype(BF)
        out_ref[:, KC:] = dot(pick, student_ref[...], ((0,), (0,))).astype(BF)
    wigf_ref[...] = wig_ref[...].astype(F32)
    rows_ref[...] = jnp.zeros_like(rows_ref)
    for degree in range(LMAX + 1):
        span = 2 * degree + 1
        row = OFFSET[degree] + min(degree, MMAX) * span
        rows_ref[degree * degree : degree * degree + span] = wigf_ref[row : row + span]
    rows_ref[49:50] = src_ref[...].astype(F32)
    rows_ref[50:51] = live_dst(dst_ref[...], count_ref[0])
    edges = rows_ref[...].astype(BF)
    for r in range(4):
        meta_ref[r, :224] = m0_ref[...]
        meta_ref[r, 224:352] = basis_ref[...]
        meta_ref[r, 352:] = edges


def live_dst(dst_row, count):
    return jnp.where(live_row(count), dst_row, EXT).astype(F32)


def pack_body(
    m0_hbm, m1_hbm, m2_hbm, student_hbm, wsrc_hbm, wdst_hbm, wout_hbm, wrad_hbm, whead_hbm,
    radial_hbm, low_ref, high_ref, bundle_hbm, m0_ref, m1_ref, m2_ref, sems,
):
    copies = fetch(
        (
            (m0_hbm, m0_ref), (m1_hbm, m1_ref), (m2_hbm, m2_ref),
            (student_hbm, bundle_hbm.at[0:32]), (wsrc_hbm, bundle_hbm.at[32:288]),
            (wdst_hbm, bundle_hbm.at[288:544]), (wout_hbm, bundle_hbm.at[544:800]),
            (wrad_hbm, bundle_hbm.at[800:928]),
            (whead_hbm.at[:C], bundle_hbm.at[928:1056, :C]),
            (whead_hbm.at[C:], bundle_hbm.at[928:1056, C:]),
            (radial_hbm, bundle_hbm.at[1056:1184, :C]),
            (radial_hbm, bundle_hbm.at[1056:1184, C:]),
        ),
        sems,
    )
    at = 0
    for part, wide, high, ready in (
        (m0_ref, 7, 224, 0), (m1_ref.at[0], 6, 192, 1), (m1_ref.at[1], 6, 192, None),
        (m2_ref.at[0], 5, 160, 2), (m2_ref.at[1], 5, 160, None),
    ):
        if ready is not None:
            copies[ready].wait()
        for n in range(wide):
            block = part[:, n * C : (n + 1) * C]
            if at < LOW:
                low_ref[at : at + high] = block
            else:
                high_ref[at - LOW : at - LOW + high] = block
            at += high
    for copy in copies[3:]:
        copy.wait()


def coefficients(refs, degree):
    parts = []
    for j in range(2 * degree + 1):
        lo = (degree * degree + j) * C
        parts += [ref[:, lo : lo + C] for ref in refs]
    return jnp.concatenate(parts, axis=0)


def gain_of(basis, radial):
    return dot(radial, basis.astype(F32).T.astype(BF), ((0,), (0,)))


def keep_turned(pack_ref, block, start, part, base):
    row = 0
    while row < C:
        which = (start + row) // part
        inside = (start + row) % part
        size = min(C - row, part - inside)
        pack_ref[which, base + inside : base + inside + size] = block[row : row + size]
        row += size


def early_body(
    inv_atoms, atoms_ref, rep_ref, meta_ref, bundle_ref, teacher_ref, left_ref, right_ref,
    grad_ref,
    turn_ref, rotated_ref, hidden_ref, ssrc_ref, sdst_ref, target_ref,
):
    student_ref = bundle_ref.at[0:32]
    wsrc_ref = bundle_ref.at[32:288]
    wdst_ref = bundle_ref.at[288:544]
    wout_ref = bundle_ref.at[544:800]
    wrad_ref = bundle_ref.at[800:928]
    head = jnp.concatenate([bundle_ref[928:1056, :C], bundle_ref[928:1056, C:]], axis=0)
    radial_ref = bundle_ref.at[1056:1184, :C]
    edges = [meta_ref[q, 352:416].astype(F32) for q in range(4)]
    ext_rows = lax.broadcasted_iota(jnp.int32, (EXT, EDGE), 0).astype(F32)
    sources = [(edges[q][49:50] == ext_rows).astype(F32) for q in range(4)]
    targets = [(edges[q][50:51] == ext_rows[:OWN]).astype(F32) for q in range(4)]
    gains = jnp.concatenate(
        [gain_of(meta_ref[q, 224:352], radial_ref[...]) for q in range(4)], axis=1
    )
    for degree in range(LMAX + 1):
        span = 2 * degree + 1
        for q in range(4):
            for j in range(span):
                row = degree * degree + j
                turn_ref[j * EXT : (j + 1) * EXT, q * EDGE : (q + 1) * EDGE] = (
                    sources[q] * edges[q][row : row + 1]
                ).astype(BF)
        stacked = coefficients((teacher_ref, left_ref, right_ref), degree)
        turned = dot(stacked, turn_ref[: span * EXT], ((0,), (0,)))
        rotated_ref[degree * C : (degree + 1) * C] = (turned * gains).astype(BF)
    column = jnp.concatenate([meta_ref[q, :224] for q in range(4)], axis=0)
    invariant = dot(column, rotated_ref[...], ((0,), (0,))).astype(BF)
    scatter = jnp.concatenate([targets[q] * edges[q][0:1] for q in range(4)], axis=1).astype(BF)
    invariants = dot(scatter, invariant, ((1,), (1,)))
    student_ext = jnp.concatenate(
        [student_ref[...], left_ref[:, KC:], right_ref[:, KC:]], axis=0
    )
    basis = jnp.concatenate([meta_ref[q, 224:352] for q in range(4)], axis=0)
    source = jnp.concatenate(sources, axis=1).astype(BF)
    onehot = jnp.concatenate(targets, axis=1).astype(BF)
    ssrc = dot(source, student_ext, ((0,), (0,))).astype(BF)
    sdst = dot(onehot, student_ref[...], ((0,), (0,))).astype(BF)
    hidden = dot(ssrc, wsrc_ref[...]) + dot(sdst, wdst_ref[...]) + dot(basis, wrad_ref[...])
    gated = (hidden * jax.nn.sigmoid(hidden)).astype(BF)
    hidden_ref[...] = hidden
    ssrc_ref[...] = ssrc
    sdst_ref[...] = sdst
    for q in range(4):
        target_ref[q] = targets[q].astype(BF)

    inv_degree = 1.0 / math.sqrt(DEG)
    target = (teacher_ref[:, :C].astype(F32) + inv_degree * invariants).astype(BF)
    pooled = (dot(onehot, gated) * inv_degree).astype(BF)
    updated = (student_ref[...].astype(F32) + dot(pooled, wout_ref[...])).astype(BF)
    predicted = dot(updated, head)
    rows = lax.broadcasted_iota(jnp.int32, (OWN, 1), 0)
    residual = jnp.where(rows < atoms_ref[0], predicted - target.astype(F32), 0.0)
    scaled = (residual * inv_atoms).astype(BF)
    upstream = dot(scaled, head, ((1,), (1,))).astype(BF)
    rep = rep_ref[0]
    mine = (rows >= rep * 8) & (rows < rep * 8 + 8)
    scaled_part = jnp.where(mine, scaled.astype(F32), 0.0).astype(BF)
    upstream_part = jnp.where(mine, upstream.astype(F32), 0.0).astype(BF)
    grad_head = dot(updated, scaled_part, ((0,), (0,)))
    grad_out = dot(pooled, upstream_part, ((0,), (0,)))
    pooled_grad = dot(upstream, wout_ref[...], ((1,), (1,))).astype(BF)
    own = pl.ds(pl.multiple_of(rep * EDGE, EDGE), EDGE)
    edge_grad = dot(target_ref[rep], pooled_grad, ((0,), (0,))) * inv_degree
    hidden = hidden_ref[own, :]
    logistic = jax.nn.sigmoid(hidden)
    hidden_grad = (edge_grad * logistic * (1.0 + hidden * (1.0 - logistic))).astype(BF)
    high = grad_ref.shape[1]
    for start, stop, value in (
        (0, 256, dot(ssrc_ref[own, :], hidden_grad, ((0,), (0,)))),
        (256, 512, dot(sdst_ref[own, :], hidden_grad, ((0,), (0,)))),
        (512, 768, grad_out),
        (768, 896, dot(meta_ref[rep, 224:352], hidden_grad, ((0,), (0,)))),
        (896, 1024, jnp.concatenate([grad_head[:C], grad_head[C:]], axis=1)),
    ):
        grad_ref[start // high : stop // high] = value.astype(BF).reshape(-1, high, SW)


def rotate_body(count_ref, rep_ref, *refs):
    raw = refs[:8]
    after_ref, keep_ref, give_ref = refs[8:11]
    held = refs[11:19]
    pack_ref, wigf_ref, turn_ref, sems = refs[19:]
    teacher_ref, left_ref, right_ref, wig_ref, basis_ref, radial_ref, src_ref, dst_ref = held
    for copy in fetch(tuple(zip(raw, held)), sems):
        copy.wait()
    rep = rep_ref[0]
    wigf_ref[:235] = wig_ref[...].astype(F32)
    wigf_ref[235:] = jnp.broadcast_to(live_dst(dst_ref[...], count_ref[0]), (5, EDGE))
    source = (src_ref[...] == lax.broadcasted_iota(jnp.int32, (EXT, EDGE), 0)).astype(F32)
    gain = gain_of(basis_ref[...], radial_ref[...])
    for degree in range(LMAX + 1):
        cap = min(degree, MMAX)
        span = 2 * degree + 1
        orders = 2 * cap + 1
        for morder in range(orders):
            for j in range(span):
                row = OFFSET[degree] + morder * span + j
                turn_ref[j * EXT : (j + 1) * EXT, morder * EDGE : (morder + 1) * EDGE] = (
                    source * wigf_ref[row : row + 1, :]
                ).astype(BF)
        stacked = coefficients((teacher_ref, left_ref, right_ref), degree)
        turned = dot(stacked, turn_ref[: span * EXT, : orders * EDGE], ((0,), (0,)))
        for morder in range(orders):
            block = (turned[:, morder * EDGE : (morder + 1) * EDGE] * gain).astype(BF)
            signed = morder - cap
            part, base = SECTIONS[signed]
            keep_turned(pack_ref, block, (degree - abs(signed)) * C, part, base)
    edges = wigf_ref[...].astype(BF)
    for out_ref, first in ((keep_ref, 0), (give_ref, 1)):
        out_ref[:928] = pack_ref[rep ^ first]
        out_ref[928:1856] = pack_ref[rep ^ (first + 2)]
        out_ref[1856:] = edges


def spread_body(parts_ref, *refs):
    out_ref = refs[-1]
    total = parts_ref[0].astype(F32)
    for i in range(1, parts_ref.shape[0]):
        total += parts_ref[i].astype(F32)
    total = total.astype(out_ref.dtype)
    for i in range(out_ref.shape[0]):
        out_ref[i] = total


def unpack_body(all_ref, src_ref, dst_ref, radial_ref, out_ref, head_ref):
    values = all_ref[...].astype(F32).reshape(1024, SW)
    src_ref[...] = values[:256]
    dst_ref[...] = values[256:512]
    out_ref[...] = values[512:768]
    radial_ref[...] = values[768:896]
    head_ref[:C] = values[896:, :C]
    head_ref[C:] = values[896:, C:]


def blocks(ref, at, count, high):
    return jnp.concatenate(
        [ref[at + n * high : at + (n + 1) * high] for n in range(count)], axis=1
    )


def mix_body(
    rep_ref, keep_ref, got_ref, low_ref, high_ref, far_low_ref, far_high_ref, after_ref,
    o0_ref, o1_ref, o2_ref, o3_ref,
    wigf_ref, back_ref, sums_ref,
):
    rep = rep_ref[0]
    groups = (keep_ref, got_ref)
    own_rows = lax.broadcasted_iota(jnp.int32, (OWN, EDGE), 0).astype(F32)
    targets = []
    for g in range(2):
        wigf_ref[g] = groups[g][1856:].astype(F32)
        targets.append((wigf_ref[g, 235:236] == own_rows).astype(F32))
    lows = (low_ref, far_low_ref)
    highs = (high_ref, far_high_ref)
    over = ((0,), (0,))

    def rows(k, base, size):
        at = 928 * k + base
        return [group[at : at + size] for group in groups]

    y0 = 0.0
    for k in range(2):
        y0 += dot(jnp.concatenate(rows(k, 0, 224), axis=1), blocks(lows[k], 0, 7, 224), over)
    y0 = y0.astype(BF)
    mixed = [None]
    both = 2 * EDGE
    for wide, base in ((6, 224), (5, 608)):
        size = wide * 32
        real = 0.0
        imag = 0.0
        for k in range(2):
            pair = jnp.concatenate(rows(k, base, size) + rows(k, base + size, size), axis=1)
            if wide == 6:
                first = blocks(lows[k], 1568, 6, 192)
                second = blocks(highs[k], 0, 6, 192)
            else:
                first = blocks(highs[k], 1152, 5, 160)
                second = blocks(highs[k], 1952, 5, 160)
            real += dot(pair, first, over)
            imag += dot(pair, second, over)
        plus = (real[:both] - imag[both:]).astype(BF)
        minus = (imag[:both] + real[both:]).astype(BF)
        mixed.append((plus, minus))
    for degree in range(LMAX + 1):
        cap = min(degree, MMAX)
        span = 2 * degree + 1
        orders = 2 * cap + 1
        stacked = []
        for morder in range(orders):
            signed = morder - cap
            if signed == 0:
                stacked.append(y0[:, degree * C : (degree + 1) * C])
            else:
                slot = degree - abs(signed)
                part = mixed[abs(signed)][0 if signed > 0 else 1]
                stacked.append(part[:, slot * C : (slot + 1) * C])
            for j in range(span):
                row = OFFSET[degree] + morder * span + j
                for g in range(2):
                    lane = morder * both + g * EDGE
                    back_ref[j * OWN : (j + 1) * OWN, lane : lane + EDGE] = (
                        targets[g] * wigf_ref[g, row : row + 1, :]
                    ).astype(BF)
        summed = dot(
            back_ref[: span * OWN, : orders * both], jnp.concatenate(stacked, axis=0)
        )
        for j in range(span):
            lo = (degree * degree + j) * C
            sums_ref[:, lo : lo + C] = summed[j * OWN : (j + 1) * OWN]
    for k, out_ref in enumerate((o0_ref, o1_ref, o2_ref, o3_ref)):
        start = pl.multiple_of((rep ^ k) * 8, 8)
        out_ref[...] = sums_ref[pl.ds(start, 8), :].astype(out_ref.dtype)


def finish_body(own_ref, s0_ref, s1_ref, s2_ref, s3_ref, out_ref):
    total = (s0_ref[...] + s1_ref[...].astype(F32)) + (
        s2_ref[...].astype(F32) + s3_ref[...].astype(F32)
    )
    out_ref[...] = (own_ref[...].astype(F32) + total * (1.0 / math.sqrt(DEG))).astype(BF)


def call(body, outs, ins, scratch=(), scalars=0, raws=0, after=0, flops=0, room=24 << 10, outs_hbm=0):
    specs = [SMEM] * scalars + [VMEM] * (len(ins) - scalars - raws - after)
    return pl.pallas_call(
        body,
        out_shape=tuple(jax.ShapeDtypeStruct(shape, dtype) for shape, dtype in outs),
        in_specs=specs + [HBM] * raws + [ANY] * after,
        out_specs=(VMEM,) * (len(outs) - outs_hbm) + (HBM,) * outs_hbm,
        scratch_shapes=list(scratch),
        compiler_params=pltpu.CompilerParams(vmem_limit_bytes=(FULL - room) << 10),
        cost_estimate=pl.CostEstimate(flops=flops, bytes_accessed=4096, transcendentals=0),
    )(*ins)


def held(arrays):
    return [pltpu.VMEM(array.shape, array.dtype) for array in arrays]


def shifted(x, axes, by):
    length = lax.axis_size(axes)
    return lax.ppermute(x, axes, [(i, (i + by) % length) for i in range(length)])


def to_brick(x, by):
    reps = lax.axis_size(REP)
    length = lax.axis_size(BRICK) * reps
    half = reps // 2
    pairs = [(i, (i + by * reps) % length // reps * reps + (i + half) % reps) for i in range(length)]
    return lax.ppermute(x, BRICK + REP, pairs)


def swapped(x, axes, mask):
    return lax.ppermute(x, axes, [(i, i ^ mask) for i in range(lax.axis_size(axes))])


def exchange(x, axes):
    return lax.all_to_all(x, axes, 0, 0, tiled=True)


def per_device(
    teacher_in, student_in, wigner, edge_basis, teacher_radial, so2_m0, so2_m1, so2_m2,
    w_src, w_dst, w_radial, w_out, w_head, src, dst, edge_count, atom_count, send_idx,
):
    bricks = lax.axis_size(BRICK)
    plane = lax.axis_size(PLANE)
    line = lax.axis_size("z")
    rep = lax.axis_index(REP).astype(jnp.int32)
    rep1 = rep.reshape(1)
    src_row = src.reshape(1, EDGE)
    dst_row = dst.reshape(1, EDGE)
    chunk = 1024 // plane
    raw = (send_idx, teacher_in, student_in, so2_m0, edge_basis, wigner, src_row, dst_row)
    to_next, to_prev, own_meta = call(
        start_body,
        [((16, KC + SW), BF), ((16, KC + SW), BF), ((4, 416, C), BF)],
        (edge_count, *raw),
        held(raw[:3])
        + [pltpu.VMEM((224, C), BF)]
        + held(raw[4:])
        + [
            pltpu.VMEM((235, EDGE), F32), pltpu.VMEM((64, EDGE), F32),
            pltpu.SemaphoreType.DMA((8,)),
        ],
        scalars=1,
        raws=8,
        room=1024,
    )
    from_left = to_brick(to_next, 1)
    from_right = to_brick(to_prev, -1)
    meta = exchange(own_meta, REP)
    mixings = (so2_m0, so2_m1, so2_m2)
    raw = (*mixings, student_in, w_src, w_dst, w_out, w_radial, w_head, teacher_radial)
    low, high, bundle = call(
        pack_body,
        [((LOW, C), BF), ((HIGH, C), BF), ((1184, SW), BF)],
        raw,
        held(mixings) + [pltpu.SemaphoreType.DMA((12,))],
        raws=10,
        flops=1 << 30,
        room=1024,
        outs_hbm=1,
    )
    (grads,) = call(
        functools.partial(early_body, 1.0 / (OWN * bricks)),
        [((plane, chunk, SW), BF)],
        (atom_count, rep1, meta, bundle, teacher_in, from_left, from_right),
        [
            pltpu.VMEM((13 * EXT, 4 * EDGE), BF), pltpu.VMEM((896, 4 * EDGE), BF),
            pltpu.VMEM((4 * EDGE, SW), F32), pltpu.VMEM((4 * EDGE, SW), BF),
            pltpu.VMEM((4 * EDGE, SW), BF), pltpu.VMEM((4, OWN, EDGE), BF),
        ],
        scalars=2,
        flops=1 << 31,
        room=12288,
    )
    low, high, grads = lax.optimization_barrier((low, high, grads))
    across_low = shifted(low, ("yh", "yl"), 1)
    across_high = shifted(high, ("yh", "yl"), -1)
    plane_parts = exchange(grads, PLANE)
    raw = (
        teacher_in, from_left, from_right, wigner, edge_basis, teacher_radial, src_row, dst_row
    )
    keep, give = call(
        rotate_body,
        [((1856 + 240, EDGE), BF)] * 2,
        (edge_count, rep1, *raw, grads),
        held(raw)
        + [
            pltpu.VMEM((4, 928, EDGE), BF), pltpu.VMEM((240, EDGE), F32),
            pltpu.VMEM((13 * EXT, 5 * EDGE), BF), pltpu.SemaphoreType.DMA((8,)),
        ],
        scalars=2,
        raws=8,
        after=1,
        flops=1 << 31,
        room=4096,
    )
    got = swapped(give, "core", 1)
    plane_parts, keep = lax.optimization_barrier((plane_parts, keep))
    (plane_sum,) = call(spread_body, [((line, chunk, SW), BF)], (plane_parts,))
    shares = call(
        mix_body,
        [((8, KC), F32)] + [((8, KC), BF)] * 3,
        (rep1, keep, got, low, high, across_low, across_high, plane_sum),
        [
            pltpu.VMEM((2, 240, EDGE), F32),
            pltpu.VMEM((13 * OWN, 10 * EDGE), BF),
            pltpu.VMEM((OWN, KC), F32),
        ],
        scalars=1,
        after=1,
        flops=1 << 32,
    )
    line_parts = exchange(plane_sum, "z")
    line_parts, share = lax.optimization_barrier((line_parts, shares[0]))
    (total,) = call(spread_body, [((plane, chunk, SW), BF)], (line_parts,))
    arrived = [share] + [swapped(shares[k], REP, k) for k in (1, 2, 3)]
    totals = exchange(total, PLANE)
    arrived = [share] + [swapped(shares[k], REP, k) for k in (1, 2, 3)]
    mine = lax.dynamic_slice_in_dim(teacher_in, rep * 8, 8, 0)
    (teacher_out,) = call(finish_body, [((8, KC), BF)], (mine, *arrived))
    grads_out = call(
        unpack_body,
        [((256, SW), F32), ((256, SW), F32), ((128, SW), F32), ((256, SW), F32), ((256, C), F32)],
        (totals,),
    )
    return (teacher_out, *grads_out)


def solution(mesh):
    fine = Mesh(mesh.devices.reshape(16, 4, 2, 2, 2), BRICK + REP)
    every = BRICK + REP
    placed = (
        P(BRICK, None),
        P(BRICK, None),
        P(None, every),
        P(every, None),
        P(),
        P(REP, None),
        P(None, REP, None),
        P(None, REP, None),
        P(),
        P(),
        P(),
        P(),
        P(),
        P(every),
        P(every),
        P(every),
        P(BRICK),
        P(BRICK, None, None),
    )
    return jax.shard_map(
        per_device,
        mesh=fine,
        in_specs=placed,
        out_specs=(P(every, None), P(), P(), P(), P(), P()),
        check_vma=False,
    )
```

```python
import functools
import math

import jax
import jax.numpy as jnp
from jax import lax
from jax.experimental import pallas as pl
from jax.experimental.pallas import tpu as pltpu
from jax.sharding import Mesh, PartitionSpec as P

LMAX = 6
MMAX = 2
DEG = 16
C = 128
OWN = 32
EXT = 64
EDGE = 128
SW = 256
KC = 6272
FULL = 64 << 10
LOW = 7 * 224 + 6 * 192
HIGH = 6 * 192 + 10 * 160
SECTIONS = {0: (224, 0), 1: (192, 224), -1: (192, 416), 2: (160, 608), -2: (160, 768)}
BF = jnp.bfloat16
F32 = jnp.float32
BRICK = ("z", "x", "yh")
REP = ("yl", "core")
PLANE = ("x", "yh", "yl", "core")
VMEM = pl.BlockSpec(memory_space=pltpu.VMEM)
HBM = pl.BlockSpec(memory_space=pltpu.HBM)
ANY = pl.BlockSpec(memory_space=pl.ANY)
SMEM = pl.BlockSpec(memory_space=pltpu.SMEM)


def offsets():
    found = []
    row = 0
    for degree in range(LMAX + 1):
        found.append(row)
        row += (2 * min(degree, MMAX) + 1) * (2 * degree + 1)
    return found


OFFSET = offsets()


def dot(left, right, over=((1,), (0,))):
    return lax.dot_general(left, right, (over, ((), ())), preferred_element_type=F32)


def live_row(count):
    return lax.broadcasted_iota(jnp.int32, (1, EDGE), 1) < count


def fetch(pairs, sems):
    copies = [
        pltpu.make_async_copy(source, target, sems.at[i])
        for i, (source, target) in enumerate(pairs)
    ]
    for copy in copies:
        copy.start()
    return copies


def start_body(
    count_ref, lists_hbm, teacher_hbm, student_hbm, m0_hbm, basis_hbm, wig_hbm, src_hbm, dst_hbm,
    next_ref, prev_ref, meta_ref,
    lists_ref, teacher_ref, student_ref, m0_ref, basis_ref, wig_ref, src_ref, dst_ref,
    wigf_ref, rows_ref, sems,
):
    copies = fetch(
        (
            (lists_hbm, lists_ref), (teacher_hbm, teacher_ref), (student_hbm, student_ref),
            (m0_hbm.at[:, :C], m0_ref), (basis_hbm, basis_ref), (wig_hbm, wig_ref),
            (src_hbm, src_ref), (dst_hbm, dst_ref),
        ),
        sems,
    )
    for copy in copies:
        copy.wait()
    rows = lax.broadcasted_iota(jnp.int32, (OWN, 16), 0)
    for k, out_ref in enumerate((next_ref, prev_ref)):
        pick = (rows == lists_ref[0, k : k + 1, :]).astype(F32).astype(BF)
        out_ref[:, :KC] = dot(pick, teacher_ref[...], ((0,), (0,))).astype(BF)
        out_ref[:, KC:] = dot(pick, student_ref[...], ((0,), (0,))).astype(BF)
    wigf_ref[...] = wig_ref[...].astype(F32)
    rows_ref[...] = jnp.zeros_like(rows_ref)
    for degree in range(LMAX + 1):
        span = 2 * degree + 1
        row = OFFSET[degree] + min(degree, MMAX) * span
        rows_ref[degree * degree : degree * degree + span] = wigf_ref[row : row + span]
    rows_ref[49:50] = src_ref[...].astype(F32)
    rows_ref[50:51] = live_dst(dst_ref[...], count_ref[0])
    edges = rows_ref[...].astype(BF)
    for r in range(4):
        meta_ref[r, :224] = m0_ref[...]
        meta_ref[r, 224:352] = basis_ref[...]
        meta_ref[r, 352:] = edges


def live_dst(dst_row, count):
    return jnp.where(live_row(count), dst_row, EXT).astype(F32)


def pack_body(
    m0_hbm, m1_hbm, m2_hbm, student_hbm, wsrc_hbm, wdst_hbm, wout_hbm, wrad_hbm, whead_hbm,
    radial_hbm, low_ref, high_ref, bundle_ref, m0_ref, m1_ref, m2_ref, sems,
):
    copies = fetch(
        (
            (m0_hbm, m0_ref), (m1_hbm, m1_ref), (m2_hbm, m2_ref),
            (student_hbm, bundle_ref.at[0:32]), (wsrc_hbm, bundle_ref.at[32:288]),
            (wdst_hbm, bundle_ref.at[288:544]), (wout_hbm, bundle_ref.at[544:800]),
            (wrad_hbm, bundle_ref.at[800:928]),
            (whead_hbm.at[:C], bundle_ref.at[928:1056, :C]),
            (whead_hbm.at[C:], bundle_ref.at[928:1056, C:]),
            (radial_hbm, bundle_ref.at[1056:1184, :C]),
            (radial_hbm, bundle_ref.at[1056:1184, C:]),
        ),
        sems,
    )
    at = 0
    for part, wide, high, ready in (
        (m0_ref, 7, 224, 0), (m1_ref.at[0], 6, 192, 1), (m1_ref.at[1], 6, 192, None),
        (m2_ref.at[0], 5, 160, 2), (m2_ref.at[1], 5, 160, None),
    ):
        if ready is not None:
            copies[ready].wait()
        for n in range(wide):
            block = part[:, n * C : (n + 1) * C]
            if at < LOW:
                low_ref[at : at + high] = block
            else:
                high_ref[at - LOW : at - LOW + high] = block
            at += high
    for copy in copies[3:]:
        copy.wait()


def coefficients(refs, degree):
    parts = []
    for j in range(2 * degree + 1):
        lo = (degree * degree + j) * C
        parts += [ref[:, lo : lo + C] for ref in refs]
    return jnp.concatenate(parts, axis=0)


def gain_of(basis, radial):
    return dot(radial, basis.astype(F32).T.astype(BF), ((0,), (0,)))


def keep_turned(pack_ref, block, start, part, base):
    row = 0
    while row < C:
        which = (start + row) // part
        inside = (start + row) % part
        size = min(C - row, part - inside)
        pack_ref[which, base + inside : base + inside + size] = block[row : row + size]
        row += size


def early_body(
    inv_atoms, atoms_ref, rep_ref, meta_ref, bundle_ref, teacher_ref, left_ref, right_ref,
    grad_ref,
    turn_ref, rotated_ref, hidden_ref, ssrc_ref, sdst_ref, target_ref,
):
    student_ref = bundle_ref.at[0:32]
    wsrc_ref = bundle_ref.at[32:288]
    wdst_ref = bundle_ref.at[288:544]
    wout_ref = bundle_ref.at[544:800]
    wrad_ref = bundle_ref.at[800:928]
    head = jnp.concatenate([bundle_ref[928:1056, :C], bundle_ref[928:1056, C:]], axis=0)
    radial_ref = bundle_ref.at[1056:1184, :C]
    edges = [meta_ref[q, 352:416].astype(F32) for q in range(4)]
    ext_rows = lax.broadcasted_iota(jnp.int32, (EXT, EDGE), 0).astype(F32)
    sources = [(edges[q][49:50] == ext_rows).astype(F32) for q in range(4)]
    targets = [(edges[q][50:51] == ext_rows[:OWN]).astype(F32) for q in range(4)]
    gains = jnp.concatenate(
        [gain_of(meta_ref[q, 224:352], radial_ref[...]) for q in range(4)], axis=1
    )
    for degree in range(LMAX + 1):
        span = 2 * degree + 1
        for q in range(4):
            for j in range(span):
                row = degree * degree + j
                turn_ref[j * EXT : (j + 1) * EXT, q * EDGE : (q + 1) * EDGE] = (
                    sources[q] * edges[q][row : row + 1]
                ).astype(BF)
        stacked = coefficients((teacher_ref, left_ref, right_ref), degree)
        turned = dot(stacked, turn_ref[: span * EXT], ((0,), (0,)))
        rotated_ref[degree * C : (degree + 1) * C] = (turned * gains).astype(BF)
    column = jnp.concatenate([meta_ref[q, :224] for q in range(4)], axis=0)
    invariant = dot(column, rotated_ref[...], ((0,), (0,))).astype(BF)
    scatter = jnp.concatenate([targets[q] * edges[q][0:1] for q in range(4)], axis=1).astype(BF)
    invariants = dot(scatter, invariant, ((1,), (1,)))
    student_ext = jnp.concatenate(
        [student_ref[...], left_ref[:, KC:], right_ref[:, KC:]], axis=0
    )
    basis = jnp.concatenate([meta_ref[q, 224:352] for q in range(4)], axis=0)
    source = jnp.concatenate(sources, axis=1).astype(BF)
    onehot = jnp.concatenate(targets, axis=1).astype(BF)
    ssrc = dot(source, student_ext, ((0,), (0,))).astype(BF)
    sdst = dot(onehot, student_ref[...], ((0,), (0,))).astype(BF)
    hidden = dot(ssrc, wsrc_ref[...]) + dot(sdst, wdst_ref[...]) + dot(basis, wrad_ref[...])
    gated = (hidden * jax.nn.sigmoid(hidden)).astype(BF)
    hidden_ref[...] = hidden
    ssrc_ref[...] = ssrc
    sdst_ref[...] = sdst
    for q in range(4):
        target_ref[q] = targets[q].astype(BF)

    inv_degree = 1.0 / math.sqrt(DEG)
    target = (teacher_ref[:, :C].astype(F32) + inv_degree * invariants).astype(BF)
    pooled = (dot(onehot, gated) * inv_degree).astype(BF)
    updated = (student_ref[...].astype(F32) + dot(pooled, wout_ref[...])).astype(BF)
    predicted = dot(updated, head)
    rows = lax.broadcasted_iota(jnp.int32, (OWN, 1), 0)
    residual = jnp.where(rows < atoms_ref[0], predicted - target.astype(F32), 0.0)
    scaled = (residual * inv_atoms).astype(BF)
    upstream = dot(scaled, head, ((1,), (1,))).astype(BF)
    rep = rep_ref[0]
    mine = (rows >= rep * 8) & (rows < rep * 8 + 8)
    scaled_part = jnp.where(mine, scaled.astype(F32), 0.0).astype(BF)
    upstream_part = jnp.where(mine, upstream.astype(F32), 0.0).astype(BF)
    grad_head = dot(updated, scaled_part, ((0,), (0,)))
    grad_out = dot(pooled, upstream_part, ((0,), (0,)))
    pooled_grad = dot(upstream, wout_ref[...], ((1,), (1,))).astype(BF)
    own = pl.ds(pl.multiple_of(rep * EDGE, EDGE), EDGE)
    edge_grad = dot(target_ref[rep], pooled_grad, ((0,), (0,))) * inv_degree
    hidden = hidden_ref[own, :]
    logistic = jax.nn.sigmoid(hidden)
    hidden_grad = (edge_grad * logistic * (1.0 + hidden * (1.0 - logistic))).astype(BF)
    high = grad_ref.shape[1]
    for start, stop, value in (
        (0, 256, dot(ssrc_ref[own, :], hidden_grad, ((0,), (0,)))),
        (256, 512, dot(sdst_ref[own, :], hidden_grad, ((0,), (0,)))),
        (512, 768, grad_out),
        (768, 896, dot(meta_ref[rep, 224:352], hidden_grad, ((0,), (0,)))),
        (896, 1024, jnp.concatenate([grad_head[:C], grad_head[C:]], axis=1)),
    ):
        grad_ref[start // high : stop // high] = value.astype(BF).reshape(-1, high, SW)


def rotate_body(count_ref, rep_ref, *refs):
    raw = refs[:8]
    after_ref, keep_ref, give_ref = refs[8:11]
    held = refs[11:19]
    pack_ref, wigf_ref, turn_ref, sems = refs[19:]
    teacher_ref, left_ref, right_ref, wig_ref, basis_ref, radial_ref, src_ref, dst_ref = held
    for copy in fetch(tuple(zip(raw, held)), sems):
        copy.wait()
    rep = rep_ref[0]
    wigf_ref[:235] = wig_ref[...].astype(F32)
    wigf_ref[235:] = jnp.broadcast_to(live_dst(dst_ref[...], count_ref[0]), (5, EDGE))
    source = (src_ref[...] == lax.broadcasted_iota(jnp.int32, (EXT, EDGE), 0)).astype(F32)
    gain = gain_of(basis_ref[...], radial_ref[...])
    for degree in range(LMAX + 1):
        cap = min(degree, MMAX)
        span = 2 * degree + 1
        orders = 2 * cap + 1
        for morder in range(orders):
            for j in range(span):
                row = OFFSET[degree] + morder * span + j
                turn_ref[j * EXT : (j + 1) * EXT, morder * EDGE : (morder + 1) * EDGE] = (
                    source * wigf_ref[row : row + 1, :]
                ).astype(BF)
        stacked = coefficients((teacher_ref, left_ref, right_ref), degree)
        turned = dot(stacked, turn_ref[: span * EXT, : orders * EDGE], ((0,), (0,)))
        for morder in range(orders):
            block = (turned[:, morder * EDGE : (morder + 1) * EDGE] * gain).astype(BF)
            signed = morder - cap
            part, base = SECTIONS[signed]
            keep_turned(pack_ref, block, (degree - abs(signed)) * C, part, base)
    edges = wigf_ref[...].astype(BF)
    for out_ref, first in ((keep_ref, 0), (give_ref, 1)):
        out_ref[:928] = pack_ref[rep ^ first]
        out_ref[928:1856] = pack_ref[rep ^ (first + 2)]
        out_ref[1856:] = edges


def spread_body(parts_ref, *refs):
    out_ref = refs[-1]
    total = parts_ref[0].astype(F32)
    for i in range(1, parts_ref.shape[0]):
        total += parts_ref[i].astype(F32)
    total = total.astype(out_ref.dtype)
    for i in range(out_ref.shape[0]):
        out_ref[i] = total


def unpack_body(all_ref, src_ref, dst_ref, radial_ref, out_ref, head_ref):
    values = all_ref[...].astype(F32).reshape(1024, SW)
    src_ref[...] = values[:256]
    dst_ref[...] = values[256:512]
    out_ref[...] = values[512:768]
    radial_ref[...] = values[768:896]
    head_ref[:C] = values[896:, :C]
    head_ref[C:] = values[896:, C:]


def blocks(ref, at, count, high):
    return jnp.concatenate(
        [ref[at + n * high : at + (n + 1) * high] for n in range(count)], axis=1
    )


def mix_body(
    rep_ref, keep_ref, got_ref, low_ref, high_ref, far_low_ref, far_high_ref, after_ref,
    o0_ref, o1_ref, o2_ref, o3_ref,
    wigf_ref, back_ref, sums_ref,
):
    rep = rep_ref[0]
    groups = (keep_ref, got_ref)
    own_rows = lax.broadcasted_iota(jnp.int32, (OWN, EDGE), 0).astype(F32)
    targets = []
    for g in range(2):
        wigf_ref[g] = groups[g][1856:].astype(F32)
        targets.append((wigf_ref[g, 235:236] == own_rows).astype(F32))
    lows = (low_ref, far_low_ref)
    highs = (high_ref, far_high_ref)
    over = ((0,), (0,))

    def rows(k, base, size):
        at = 928 * k + base
        return [group[at : at + size] for group in groups]

    y0 = 0.0
    for k in range(2):
        y0 += dot(jnp.concatenate(rows(k, 0, 224), axis=1), blocks(lows[k], 0, 7, 224), over)
    y0 = y0.astype(BF)
    mixed = [None]
    both = 2 * EDGE
    for wide, base in ((6, 224), (5, 608)):
        size = wide * 32
        real = 0.0
        imag = 0.0
        for k in range(2):
            pair = jnp.concatenate(rows(k, base, size) + rows(k, base + size, size), axis=1)
            if wide == 6:
                first = blocks(lows[k], 1568, 6, 192)
                second = blocks(highs[k], 0, 6, 192)
            else:
                first = blocks(highs[k], 1152, 5, 160)
                second = blocks(highs[k], 1952, 5, 160)
            real += dot(pair, first, over)
            imag += dot(pair, second, over)
        plus = (real[:both] - imag[both:]).astype(BF)
        minus = (imag[:both] + real[both:]).astype(BF)
        mixed.append((plus, minus))
    for degree in range(LMAX + 1):
        cap = min(degree, MMAX)
        span = 2 * degree + 1
        orders = 2 * cap + 1
        stacked = []
        for morder in range(orders):
            signed = morder - cap
            if signed == 0:
                stacked.append(y0[:, degree * C : (degree + 1) * C])
            else:
                slot = degree - abs(signed)
                part = mixed[abs(signed)][0 if signed > 0 else 1]
                stacked.append(part[:, slot * C : (slot + 1) * C])
            for j in range(span):
                row = OFFSET[degree] + morder * span + j
                for g in range(2):
                    lane = morder * both + g * EDGE
                    back_ref[j * OWN : (j + 1) * OWN, lane : lane + EDGE] = (
                        targets[g] * wigf_ref[g, row : row + 1, :]
                    ).astype(BF)
        summed = dot(
            back_ref[: span * OWN, : orders * both], jnp.concatenate(stacked, axis=0)
        )
        for j in range(span):
            lo = (degree * degree + j) * C
            sums_ref[:, lo : lo + C] = summed[j * OWN : (j + 1) * OWN]
    for k, out_ref in enumerate((o0_ref, o1_ref, o2_ref, o3_ref)):
        start = pl.multiple_of((rep ^ k) * 8, 8)
        out_ref[...] = sums_ref[pl.ds(start, 8), :].astype(out_ref.dtype)


def finish_body(own_ref, s0_ref, s1_ref, s2_ref, s3_ref, out_ref):
    total = (s0_ref[...] + s1_ref[...].astype(F32)) + (
        s2_ref[...].astype(F32) + s3_ref[...].astype(F32)
    )
    out_ref[...] = (own_ref[...].astype(F32) + total * (1.0 / math.sqrt(DEG))).astype(BF)


def call(body, outs, ins, scratch=(), scalars=0, raws=0, after=0, flops=0, room=24 << 10):
    specs = [SMEM] * scalars + [VMEM] * (len(ins) - scalars - raws - after)
    return pl.pallas_call(
        body,
        out_shape=tuple(jax.ShapeDtypeStruct(shape, dtype) for shape, dtype in outs),
        in_specs=specs + [HBM] * raws + [ANY] * after,
        out_specs=(VMEM,) * len(outs),
        scratch_shapes=list(scratch),
        compiler_params=pltpu.CompilerParams(vmem_limit_bytes=(FULL - room) << 10),
        cost_estimate=pl.CostEstimate(flops=flops, bytes_accessed=4096, transcendentals=0),
    )(*ins)


def held(arrays):
    return [pltpu.VMEM(array.shape, array.dtype) for array in arrays]


def shifted(x, axes, by):
    length = lax.axis_size(axes)
    return lax.ppermute(x, axes, [(i, (i + by) % length) for i in range(length)])


def to_brick(x, by):
    reps = lax.axis_size(REP)
    length = lax.axis_size(BRICK) * reps
    half = reps // 2
    pairs = [(i, (i + by * reps) % length // reps * reps + (i + half) % reps) for i in range(length)]
    return lax.ppermute(x, BRICK + REP, pairs)


def swapped(x, axes, mask):
    return lax.ppermute(x, axes, [(i, i ^ mask) for i in range(lax.axis_size(axes))])


def exchange(x, axes):
    return lax.all_to_all(x, axes, 0, 0, tiled=True)


def per_device(
    teacher_in, student_in, wigner, edge_basis, teacher_radial, so2_m0, so2_m1, so2_m2,
    w_src, w_dst, w_radial, w_out, w_head, src, dst, edge_count, atom_count, send_idx,
):
    bricks = lax.axis_size(BRICK)
    plane = lax.axis_size(PLANE)
    line = lax.axis_size("z")
    rep = lax.axis_index(REP).astype(jnp.int32)
    rep1 = rep.reshape(1)
    src_row = src.reshape(1, EDGE)
    dst_row = dst.reshape(1, EDGE)
    chunk = 1024 // plane
    raw = (send_idx, teacher_in, student_in, so2_m0, edge_basis, wigner, src_row, dst_row)
    to_next, to_prev, own_meta = call(
        start_body,
        [((16, KC + SW), BF), ((16, KC + SW), BF), ((4, 416, C), BF)],
        (edge_count, *raw),
        held(raw[:3])
        + [pltpu.VMEM((224, C), BF)]
        + held(raw[4:])
        + [
            pltpu.VMEM((235, EDGE), F32), pltpu.VMEM((64, EDGE), F32),
            pltpu.SemaphoreType.DMA((8,)),
        ],
        scalars=1,
        raws=8,
        room=1024,
    )
    from_left = to_brick(to_next, 1)
    from_right = to_brick(to_prev, -1)
    meta = exchange(own_meta, REP)
    mixings = (so2_m0, so2_m1, so2_m2)
    raw = (*mixings, student_in, w_src, w_dst, w_out, w_radial, w_head, teacher_radial)
    low, high, bundle = call(
        pack_body,
        [((LOW, C), BF), ((HIGH, C), BF), ((1184, SW), BF)],
        raw,
        held(mixings) + [pltpu.SemaphoreType.DMA((12,))],
        raws=10,
        flops=1 << 30,
        room=1024,
    )
    (grads,) = call(
        functools.partial(early_body, 1.0 / (OWN * bricks)),
        [((plane, chunk, SW), BF)],
        (atom_count, rep1, meta, bundle, teacher_in, from_left, from_right),
        [
            pltpu.VMEM((13 * EXT, 4 * EDGE), BF), pltpu.VMEM((896, 4 * EDGE), BF),
            pltpu.VMEM((4 * EDGE, SW), F32), pltpu.VMEM((4 * EDGE, SW), BF),
            pltpu.VMEM((4 * EDGE, SW), BF), pltpu.VMEM((4, OWN, EDGE), BF),
        ],
        scalars=2,
        flops=1 << 31,
        room=12288,
    )
    low, high, grads = lax.optimization_barrier((low, high, grads))
    across_low = shifted(low, ("yh", "yl"), 1)
    across_high = shifted(high, ("yh", "yl"), -1)
    plane_parts = exchange(grads, PLANE)
    raw = (
        teacher_in, from_left, from_right, wigner, edge_basis, teacher_radial, src_row, dst_row
    )
    keep, give = call(
        rotate_body,
        [((1856 + 240, EDGE), BF)] * 2,
        (edge_count, rep1, *raw, grads),
        held(raw)
        + [
            pltpu.VMEM((4, 928, EDGE), BF), pltpu.VMEM((240, EDGE), F32),
            pltpu.VMEM((13 * EXT, 5 * EDGE), BF), pltpu.SemaphoreType.DMA((8,)),
        ],
        scalars=2,
        raws=8,
        after=1,
        flops=1 << 31,
        room=4096,
    )
    got = swapped(give, "core", 1)
    plane_parts, keep = lax.optimization_barrier((plane_parts, keep))
    (plane_sum,) = call(spread_body, [((line, chunk, SW), BF)], (plane_parts,))
    shares = call(
        mix_body,
        [((8, KC), F32)] + [((8, KC), BF)] * 3,
        (rep1, keep, got, low, high, across_low, across_high, plane_sum),
        [
            pltpu.VMEM((2, 240, EDGE), F32),
            pltpu.VMEM((13 * OWN, 10 * EDGE), BF),
            pltpu.VMEM((OWN, KC), F32),
        ],
        scalars=1,
        after=1,
        flops=1 << 32,
    )
    line_parts = exchange(plane_sum, "z")
    line_parts, share = lax.optimization_barrier((line_parts, shares[0]))
    (total,) = call(spread_body, [((plane, chunk, SW), BF)], (line_parts,))
    arrived = [share] + [swapped(shares[k], REP, k) for k in (1, 2, 3)]
    totals = exchange(total, PLANE)
    arrived = [share] + [swapped(shares[k], REP, k) for k in (1, 2, 3)]
    mine = lax.dynamic_slice_in_dim(teacher_in, rep * 8, 8, 0)
    (teacher_out,) = call(finish_body, [((8, KC), BF)], (mine, *arrived))
    grads_out = call(
        unpack_body,
        [((256, SW), F32), ((256, SW), F32), ((128, SW), F32), ((256, SW), F32), ((256, C), F32)],
        (totals,),
    )
    return (teacher_out, *grads_out)


def solution(mesh):
    fine = Mesh(mesh.devices.reshape(16, 4, 2, 2, 2), BRICK + REP)
    every = BRICK + REP
    placed = (
        P(BRICK, None),
        P(BRICK, None),
        P(None, every),
        P(every, None),
        P(),
        P(REP, None),
        P(None, REP, None),
        P(None, REP, None),
        P(),
        P(),
        P(),
        P(),
        P(),
        P(every),
        P(every),
        P(every),
        P(BRICK),
        P(BRICK, None, None),
    )
    return jax.shard_map(
        per_device,
        mesh=fine,
        in_specs=placed,
        out_specs=(P(every, None), P(), P(), P(), P(), P()),
        check_vma=False,
    )
```
